128 devices in a mesh: expert: 8 (over y, core), shard: 16 (over z, x).
Axes of the slice: x: 4, y: 4, z: 4, core: 2. Of those that a mesh axis runs over, the one named last changes fastest.
Arguments:
- slot_inputs: bfloat16 [32768, 4096], P(('expert', 'shard')), may hold values from -6 to 6
- slot_grads: bfloat16 [32768, 8192], P(('expert', 'shard')), may hold values from -6 to 6
- slot_expert: int32 [32768, 1], P(('expert', 'shard')), may hold values from 0 to 7; in each aligned block of 256 rows (0 to 255, 256 to 511, ...) at most 64 rows name the same one
- weight_grad: bfloat16 [8, 4096, 8192], P('expert', None, 'shard'), may hold values from -6 to 6
Outputs:
- preconditioned: bfloat16 [8, 4096, 8192], P('expert', None, 'shard')
The draws below stay inside these ranges and needn't reach their ends.
Inputs may be any that keep to these rules, and one draw needn't show every extreme that they name: `slot_expert`: among the slots of one device no expert appears more than 64 times, and some expert appears exactly 64 times on some device; every expert appears somewhere.
All inputs are finite; a program needn't handle non-finite values.
Results may differ from the reference program's by a relative error of at most 0.01.
Values may be sent and summed in bfloat16 or wider, within the bound.
No kernel may reach another device: no remote copies, remote signals or barrier semaphores. Data moves between devices by JAX's collectives and lax.ppermute only.
A program may use at most 128 MiB of HBM per device.

```python
import math
import jax
import jax.numpy as jnp
import numpy as np
from jax import lax

D = 4096
FF = 8192
BLK = 512
NS_STEPS = 8
SLOT_DEV = 256
EXPERTS = 8
CAP = 64
SLOTS = 32768
N_EXPERT = 8
N_SHARD = 16


def steps_of(rng, shape, cuts, low, high):
    loudness, own = 1.0, jax.random.fold_in(rng, 6)
    for dim, blocks in cuts:
        draws = jnp.exp(jax.random.uniform(jax.random.fold_in(own, dim), (blocks,), jnp.float32, low / len(cuts), high / len(cuts)))
        loudness = loudness * jnp.repeat(draws, shape[dim] // blocks).reshape([-1 if axis == dim else 1 for axis in range(len(shape))])
    return loudness


def deal_out(stream_key, own, number, rows, number_of, top, reach, slope):
    order = jax.random.permutation(stream_key, number_of)
    crowded, common = load_shares(number_of, rows * top, reach, slope, True), load_shares(number_of, rows * top, reach, slope, False)
    places = jnp.arange(number_of)

    def named(sizes, rotation):
        used = int((sizes > 0).sum())
        fixed = max(1, used // 4)
        passed = fixed + (places - fixed + rotation * (used - fixed)) % max(1, number_of - fixed)
        return jnp.zeros((number_of,), jnp.int32).at[order[jnp.where(places < fixed, places, passed)]].set(jnp.asarray(sizes, jnp.int32))

    sizes = jnp.where(number % 4 == 0, named(crowded, number // 4), named(common, number - number // 4 - 1))
    mixed = jax.random.permutation(jax.random.fold_in(own, 3), number_of)
    source_of, receiver = mixed[0:number_of // 2 * 2:2], mixed[1:number_of // 2 * 2:2]
    room = jnp.minimum(sizes[source_of] - 1, reach - sizes[receiver]) // 2
    room = jnp.where((source_of == order[0]) | (receiver == order[0]) | (sizes[receiver] == 0), 0, jnp.maximum(room, 0))
    passed = jax.random.randint(jax.random.fold_in(own, 4), (number_of // 2,), 0, 1 << 20) % (room + 1)
    sizes = sizes.at[source_of].add(-passed).at[receiver].add(passed)
    items = jnp.searchsorted(jnp.cumsum(sizes), jnp.arange(rows * top), side="right").astype(jnp.int32)
    listing = items.reshape(top, rows).T
    listing = listing[jax.random.permutation(jax.random.fold_in(own, 1), rows)]
    rotation = jax.random.randint(jax.random.fold_in(own, 2), (rows, 1), 0, top)
    return jnp.take_along_axis(listing, (jnp.arange(top)[None, :] + rotation) % top, axis=1)


def load_shares(count, total, most, skew, full):
    loads = [(1 << 20) // math.isqrt(rank ** skew) + 1 for rank in range(1, count + 1)]
    largest = most if full else min(most, max(-(-total // count), total * loads[0] // sum(loads)))
    least = 1 if total - largest >= count - 1 else 0
    given, spare = [largest] + [least] * (count - 1), total - largest - least * (count - 1)
    while spare > 0:
        movable = [i for i in range(1, count) if given[i] < largest] or [i for i in range(1, count) if given[i] < most]
        whole, remaining = sum([loads[i] for i in movable]), spare
        for i in movable:
            addition = min(most - given[i], max(1, remaining * loads[i] // whole), spare)
            given[i] = given[i] + addition
            spare = spare - addition
    return np.array(given)


def bell_draw(own_key, shape, spread, reach, shards=(), kind=jnp.bfloat16):
    entries = jax.random.normal(own_key, shape, jnp.float32) * spread
    if len(shards) > 0:
        entries = steps_of(own_key, shape, shards, -0.22, 0.18) * entries
    return jnp.clip(entries, min=-reach, max=reach).astype(kind)


def setup_inputs(seed: int = 0) -> dict:
    splits = jax.random.split(jax.random.key(seed), 5)
    slot_inputs = bell_draw(splits[0], (SLOTS, D), 1.0, 6.0, ((0, 128),))
    slot_grads = bell_draw(splits[1], (SLOTS, FF), 1.0, 6.0, ((0, 128),))
    slot_expert_keys = jax.random.split(jax.random.fold_in(splits[2], 1), SLOTS // SLOT_DEV)
    slot_expert_turns = jax.random.permutation(jax.random.fold_in(splits[2], 3), SLOTS // SLOT_DEV)
    slot_expert = jax.vmap(lambda own, number: deal_out(jax.random.fold_in(splits[2], 2), own, number, SLOT_DEV, EXPERTS, 1, CAP, 2))(slot_expert_keys, slot_expert_turns).reshape((SLOTS, 1))
    weight_grad = bell_draw(splits[3], (EXPERTS, D, FF), 1.0, 6.0, ((0, 8), (2, 16)))
    return {"slot_inputs": slot_inputs, "slot_grads": slot_grads, "slot_expert": slot_expert, "weight_grad": weight_grad}


DAMPING = 0.1
PRECISE = lax.Precision.HIGHEST

def slot_sources(route_ids):
    labels = jnp.arange(EXPERTS, dtype=jnp.int32)
    onehot = (route_ids[:, None] == labels[None, :]).astype(jnp.int32)
    before = jnp.cumsum(onehot, axis=0) - onehot
    placed = route_ids * CAP + lax.optimization_barrier(jnp.sum(before * onehot, axis=1))
    target = jnp.arange(EXPERTS * CAP, dtype=jnp.int32)
    matched = (placed[None, :] == target[:, None]).astype(jnp.int32)
    source = lax.optimization_barrier(jnp.sum(matched * jnp.arange(SLOT_DEV, dtype=jnp.int32)[None, :], axis=1))
    return (source.astype(jnp.int32), lax.optimization_barrier(jnp.sum(matched, axis=1)))

def newton(matrix):
    extent = matrix.shape[-1]
    norm_value = jnp.sqrt(lax.optimization_barrier(jnp.sum(matrix * matrix, axis=(-2, -1), keepdims=True)))
    iterate = jnp.eye(extent, dtype=jnp.float32) / norm_value
    for step_index in range(NS_STEPS):
        product = jnp.matmul(jnp.matmul(iterate, matrix, precision=PRECISE), iterate, precision=PRECISE)
        iterate = 2.0 * iterate - product
    return iterate

def reference(slot_inputs, slot_grads, slot_expert, weight_grad):
    device_count = N_EXPERT * N_SHARD
    act_blocks = D // BLK
    out_blocks = FF // BLK
    inputs = slot_inputs.reshape(device_count, SLOT_DEV, D)
    grads = slot_grads.reshape(device_count, SLOT_DEV, FF)
    routes = slot_expert.reshape(device_count, SLOT_DEV)

    def add_device(carry, entry):
        total_act, total_out = carry
        rows_in, rows_grad, rows_route = entry
        source, filled = slot_sources(rows_route)
        keep_mask = filled.astype(jnp.float32)[:, None]
        taken_in = jnp.take(rows_in, source, axis=0).astype(jnp.float32) * keep_mask
        taken_grad = jnp.take(rows_grad, source, axis=0).astype(jnp.float32) * keep_mask
        taken_in = taken_in.reshape(EXPERTS, CAP, act_blocks, BLK)
        taken_grad = taken_grad.reshape(EXPERTS, CAP, out_blocks, BLK)
        total_act = total_act + jnp.einsum('ecbi,ecbj->ebij', taken_in, taken_in, precision=PRECISE)
        total_out = total_out + jnp.einsum('ecbi,ecbj->ebij', taken_grad, taken_grad, precision=PRECISE)
        return ((total_act, total_out), None)
    start = (jnp.zeros((EXPERTS, act_blocks, BLK, BLK), jnp.float32), jnp.zeros((EXPERTS, out_blocks, BLK, BLK), jnp.float32))
    (act_gram, out_gram), unused = lax.scan(add_device, start, (inputs, grads, routes))
    labels = jnp.arange(EXPERTS, dtype=jnp.int32)
    count = lax.optimization_barrier(jnp.sum((slot_expert[:, 0][:, None] == labels[None, :]).astype(jnp.float32), axis=0))
    identity = jnp.eye(BLK, dtype=jnp.float32)
    act_factor = act_gram / count[:, None, None, None] + DAMPING * identity
    out_factor = out_gram / count[:, None, None, None] + DAMPING * identity
    act_inverse = newton(act_factor).astype(jnp.bfloat16)
    out_inverse = newton(out_factor).astype(jnp.bfloat16)

    def apply_expert(entry):
        gradient, left_inv, right_inv = entry
        halfway = jnp.einsum('dgi,gij->dgj', gradient.reshape(D, out_blocks, BLK).astype(jnp.float32), right_inv.astype(jnp.float32), precision=PRECISE).astype(jnp.bfloat16)
        halfway = halfway.reshape(act_blocks, BLK, FF)
        result = jnp.einsum('bij,bjc->bic', left_inv.astype(jnp.float32), halfway.astype(jnp.float32), precision=PRECISE)
        return result.reshape(D, FF).astype(jnp.bfloat16)
    return lax.map(apply_expert, (weight_grad, act_inverse, out_inverse))
```

```python
import jax
import jax.numpy as jnp
from jax import lax
from jax.experimental import pallas as pl
from jax.experimental.pallas import tpu as pltpu
from jax.sharding import PartitionSpec as P

D = 4096
FF = 8192
BLK = 512
HALF = 256
TILE = 128
EXPERTS = 8
SLOT_DEV = 256
NS_STEPS = 8
DAMPING = 0.1
VMEM_LIMIT = 40 * 1024 * 1024

TILES = [(i, j) for i in range(4) for j in range(i, 4)]
PACKED = len(TILES) * TILE


def params():
    return pltpu.CompilerParams(vmem_limit_bytes=VMEM_LIMIT)


def route_kernel(interleave, col_ref, row_ref, x_ref, o_ref, perm):
    @pl.when(pl.program_id(0) == 0)
    def _():
        n = SLOT_DEV
        sub = lax.broadcasted_iota(jnp.int32, (n, n), 0)
        lane = lax.broadcasted_iota(jnp.int32, (n, n), 1)
        earlier = col_ref[...] * n + sub < row_ref[...] * n + lane
        place = jnp.sum(earlier.astype(jnp.float32), axis=0, keepdims=True)
        place = place.astype(jnp.int32)
        if interleave:
            place = (place >> 1) + (place & 1) * (n // 2)
        perm[...] = (sub == place).astype(jnp.float32).astype(jnp.bfloat16)

    moved = jnp.dot(perm[...], x_ref[...], preferred_element_type=jnp.float32)
    o_ref[...] = moved.astype(jnp.bfloat16).reshape(o_ref.shape)


def route(x, ids_col, ids_row, interleave):
    blocks = x.shape[1] // BLK
    parts = 2 if interleave else 1
    rows = SLOT_DEV // parts
    return pl.pallas_call(
        lambda *refs: route_kernel(interleave, *refs),
        grid=(blocks,),
        in_specs=[
            pl.BlockSpec((SLOT_DEV, 1), lambda b: (0, 0)),
            pl.BlockSpec((1, SLOT_DEV), lambda b: (0, 0)),
            pl.BlockSpec((SLOT_DEV, BLK), lambda b: (0, b)),
        ],
        out_specs=pl.BlockSpec((parts, rows, BLK), lambda b: (b, 0, 0)),
        out_shape=jax.ShapeDtypeStruct((blocks * parts, rows, BLK), jnp.bfloat16),
        scratch_shapes=[pltpu.VMEM((SLOT_DEV, SLOT_DEV), jnp.bfloat16)],
        compiler_params=params(),
        cost_estimate=pl.CostEstimate(
            flops=2 * SLOT_DEV * SLOT_DEV * x.shape[1],
            bytes_accessed=4 * SLOT_DEV * x.shape[1],
            transcendentals=0,
        ),
    )(ids_col, ids_row, x)


def gram_kernel(window, start_ref, end_ref, x_ref, o_ref, picked):
    e = pl.program_id(0)
    sources, rows = x_ref.shape[0], x_ref.shape[1]
    place = lax.broadcasted_iota(jnp.int32, (window, BLK), 0)
    for j in range(sources):
        start = start_ref[j, e]
        end = end_ref[j, e]
        base = pl.multiple_of(jnp.minimum(start // 16 * 16, rows - window), 16)
        part = x_ref[j, pl.ds(base, window), :]
        keep = (place >= start - base) & (place < end - base)
        picked[pl.ds(j * window, window), :] = jnp.where(keep, part, jnp.zeros_like(part))
    left = picked[:, :HALF]
    right = picked[:, HALF:]

    def product(a, b):
        return lax.dot_general(a, b, (((0,), (0,)), ((), ())), preferred_element_type=jnp.float32)

    quarters = {(0, 0): product(left, left), (0, 1): product(left, right), (1, 1): product(right, right)}
    for n, (i, j) in enumerate(TILES):
        block = quarters[(i // 2, j // 2)]
        r, c = i % 2 * TILE, j % 2 * TILE
        o_ref[0, pl.ds(n * TILE, TILE), :] = block[r : r + TILE, c : c + TILE]


def gram(x, start, end, window):
    sources, rows, _ = x.shape
    return pl.pallas_call(
        lambda *refs: gram_kernel(window, *refs),
        grid_spec=pltpu.PrefetchScalarGridSpec(
            num_scalar_prefetch=2,
            grid=(EXPERTS,),
            in_specs=[pl.BlockSpec((sources, rows, BLK), lambda e, s, t: (0, 0, 0))],
            out_specs=pl.BlockSpec((1, PACKED, TILE), lambda e, s, t: (e, 0, 0)),
            scratch_shapes=[pltpu.VMEM((sources * window, BLK), jnp.bfloat16)],
        ),
        out_shape=jax.ShapeDtypeStruct((EXPERTS, PACKED, TILE), jnp.float32),
        compiler_params=params(),
        cost_estimate=pl.CostEstimate(
            flops=2 * EXPERTS * sources * window * BLK * BLK,
            bytes_accessed=2 * x.size + 4 * EXPERTS * PACKED * TILE,
            transcendentals=0,
        ),
    )(start, end, x)


def split(x):
    high = x.astype(jnp.bfloat16)
    return high, (x - high.astype(jnp.float32)).astype(jnp.bfloat16)


def dot3(a, b):
    def one(p, q):
        return jnp.dot(p, q, preferred_element_type=jnp.float32)

    return one(a[0], b[0]) + (one(a[0], b[1]) + one(a[1], b[0]))


def newton_kernel(count_ref, *refs):
    grams, o_ref, e_ref, y_ref = refs[:-3], refs[-3], refs[-2], refs[-1]
    scale = 1.0 / count_ref[0]
    for n, (i, j) in enumerate(TILES):
        tile = grams[0][pl.ds(n * TILE, TILE), :]
        for more in grams[1:]:
            tile = tile + more[pl.ds(n * TILE, TILE), :]
        tile = tile * scale
        e_ref[pl.ds(i * TILE, TILE), pl.ds(j * TILE, TILE)] = tile
        if i != j:
            e_ref[pl.ds(j * TILE, TILE), pl.ds(i * TILE, TILE)] = tile.T
    sub = lax.broadcasted_iota(jnp.int32, (BLK, BLK), 0)
    lane = lax.broadcasted_iota(jnp.int32, (BLK, BLK), 1)
    diagonal = sub == lane
    matrix = e_ref[...] + jnp.where(diagonal, DAMPING, 0.0)
    norm = jnp.sqrt(jnp.sum(matrix * matrix, keepdims=True))
    e = matrix / norm
    e_ref[...] = e
    y_ref[...] = (jnp.where(diagonal, 2.0, 0.0) - e) / norm
    es = split(e)
    e_ref[...] = 2.0 * e_ref[...] - dot3(es, es)

    def step(_, carry):
        es = split(e_ref[...])
        ys = split(y_ref[...])
        y_ref[...] = 2.0 * y_ref[...] - dot3(ys, es)
        e_ref[...] = 2.0 * e_ref[...] - dot3(es, es)
        return carry

    lax.fori_loop(0, NS_STEPS - 2, step, 0)
    y = y_ref[...]
    o_ref[...] = (2.0 * y - dot3(split(y), split(e_ref[...]))).astype(jnp.bfloat16)


def newton(count, *grams):
    return pl.pallas_call(
        newton_kernel,
        in_specs=[pl.BlockSpec(memory_space=pltpu.SMEM)]
        + [pl.BlockSpec(memory_space=pltpu.VMEM)] * len(grams),
        out_specs=pl.BlockSpec(memory_space=pltpu.VMEM),
        out_shape=jax.ShapeDtypeStruct((BLK, BLK), jnp.bfloat16),
        scratch_shapes=[pltpu.VMEM((BLK, BLK), jnp.float32)] * 2,
        compiler_params=params(),
        cost_estimate=pl.CostEstimate(
            flops=2 * 14 * 3 * BLK**3, bytes_accessed=4 * BLK * BLK, transcendentals=0
        ),
    )(count, *grams)


def block_dot_kernel(a_ref, b_ref, o_ref):
    o_ref[...] = jnp.dot(
        a_ref[...], b_ref[...], preferred_element_type=jnp.float32
    ).astype(jnp.bfloat16)


def block_dot(a, b):
    blocks = a.shape[0] // BLK
    single = b.shape[0] == BLK
    return pl.pallas_call(
        block_dot_kernel,
        grid=(blocks,),
        in_specs=[
            pl.BlockSpec((BLK, BLK), lambda n: (n, 0)),
            pl.BlockSpec((BLK, BLK), lambda n: (0, 0) if single else (n, 0)),
        ],
        out_specs=pl.BlockSpec((BLK, BLK), lambda n: (n, 0)),
        out_shape=jax.ShapeDtypeStruct((blocks * BLK, BLK), jnp.bfloat16),
        compiler_params=params(),
        cost_estimate=pl.CostEstimate(
            flops=2 * blocks * BLK**3, bytes_accessed=6 * blocks * BLK * BLK, transcendentals=0
        ),
    )(a, b)


def per_device(slot_inputs, slot_grads, slot_expert, weight_grad):
    group_pos = lax.axis_index("expert")
    shard_pos = lax.axis_index("shard")
    labels = jnp.arange(EXPERTS, dtype=jnp.int32)
    ids_row = slot_expert.reshape(1, SLOT_DEV)
    sent_act = route(slot_inputs, slot_expert, ids_row, True)
    sent_out = route(slot_grads, slot_expert, ids_row, False)

    own_counts = jnp.sum((slot_expert == labels[None, :]).astype(jnp.int32), axis=0)
    counts = lax.all_gather(own_counts[None], ("expert", "shard"), axis=0, tiled=True)
    routed = jnp.sum(jnp.where(labels[None, :] == group_pos, counts, 0)).astype(jnp.float32)
    routed = routed.reshape(1)
    shards = lax.axis_size("shard")
    plane = lax.dynamic_slice_in_dim(counts, group_pos * shards, shards, 0)
    end = jnp.cumsum(plane, axis=1)
    start = end - plane
    odd = shard_pos & 1

    got_act = lax.all_to_all(sent_act, "shard", 0, 0, tiled=True)
    act = gram(got_act, (start + 1 - odd) >> 1, (end + 1 - odd) >> 1, 48)
    act = lax.psum_scatter(act, "expert", scatter_dimension=0, tiled=True)[0]
    got_out = lax.all_to_all(sent_out, "shard", 0, 0, tiled=True)
    out = gram(got_out, start, end, 80)
    out = lax.psum_scatter(out, "expert", scatter_dimension=0, tiled=True)[0]

    other = lax.ppermute(act, "shard", [(i, i ^ 1) for i in range(shards)])
    act_inverse = newton(routed, act, other)
    rows = lax.dynamic_slice_in_dim(act_inverse, odd * HALF, HALF, 0)
    act_inverse = lax.all_gather(rows, "shard", axis=0, tiled=True)
    out_inverse = newton(routed, out)

    left = block_dot(act_inverse, weight_grad[0])
    return block_dot(left, out_inverse)[None]


def solution(mesh):
    in_specs = (
        P(("expert", "shard"), None),
        P(("expert", "shard"), None),
        P(("expert", "shard"), None),
        P("expert", None, "shard"),
    )
    out_specs = P("expert", None, "shard")
    return jax.shard_map(
        per_device, mesh=mesh, in_specs=in_specs, out_specs=out_specs, check_vma=False
    )
```

```python
import jax
import jax.numpy as jnp
from jax import lax
from jax.experimental import pallas as pl
from jax.experimental.pallas import tpu as pltpu
from jax.sharding import PartitionSpec as P

D = 4096
FF = 8192
BLK = 512
HALF = 256
TILE = 128
EXPERTS = 8
SLOT_DEV = 256
NS_STEPS = 8
DAMPING = 0.1
VMEM_LIMIT = 20 * 1024 * 1024

TILES = [(i, j) for i in range(4) for j in range(i, 4)]
PACKED = len(TILES) * TILE
NOTE = 16
CAP = 64

BRIEF = pl.CostEstimate(flops=1 << 20, bytes_accessed=1 << 12, transcendentals=0)


def params():
    return pltpu.CompilerParams(vmem_limit_bytes=VMEM_LIMIT)


def route_kernel(noted, col_ref, row_ref, x_ref, o_ref, perm):
    n = SLOT_DEV

    @pl.when(pl.program_id(0) == 0)
    def _():
        sub = lax.broadcasted_iota(jnp.int32, (n, n), 0)
        lane = lax.broadcasted_iota(jnp.int32, (n, n), 1)
        earlier = col_ref[...] * n + sub < row_ref[...] * n + lane
        place = jnp.sum(earlier.astype(jnp.float32), axis=0, keepdims=True)
        place = place.astype(jnp.int32)
        if noted:
            place = (place >> 1) + (place & 1) * (n // 2)
        perm[...] = (sub == place).astype(jnp.float32).astype(jnp.bfloat16)

    moved = jnp.dot(perm[...], x_ref[...], preferred_element_type=jnp.float32)
    moved = moved.astype(jnp.bfloat16)
    if noted:
        lane = lax.broadcasted_iota(jnp.int32, (n, BLK), 1)
        counts = jnp.sum((col_ref[...] == lane).astype(jnp.float32), axis=0, keepdims=True)
        counts = jnp.broadcast_to(counts, (NOTE, BLK)).astype(jnp.bfloat16)
        for half in range(2):
            o_ref[half, : n // 2, :] = moved[half * (n // 2) : (half + 1) * (n // 2)]
            o_ref[half, n // 2 :, :] = counts
    else:
        o_ref[0] = moved


def route(x, ids_col, ids_row, noted):
    blocks = x.shape[1] // BLK
    block = (2, SLOT_DEV // 2 + NOTE, BLK) if noted else (1, SLOT_DEV, BLK)
    return pl.pallas_call(
        lambda *refs: route_kernel(noted, *refs),
        grid=(blocks,),
        in_specs=[
            pl.BlockSpec((SLOT_DEV, 1), lambda b: (0, 0)),
            pl.BlockSpec((1, SLOT_DEV), lambda b: (0, 0)),
            pl.BlockSpec((SLOT_DEV, BLK), lambda b: (0, b)),
        ],
        out_specs=pl.BlockSpec(block, lambda b: (b, 0, 0)),
        out_shape=jax.ShapeDtypeStruct((blocks * block[0],) + block[1:], jnp.bfloat16),
        scratch_shapes=[pltpu.VMEM((SLOT_DEV, SLOT_DEV), jnp.bfloat16)],
        compiler_params=params(),
        cost_estimate=BRIEF,
    )(ids_col, ids_row, x)


def gram_kernel(rows, window, start_ref, end_ref, x_ref, o_ref, picked):
    e = pl.program_id(0)
    place = lax.broadcasted_iota(jnp.int32, (window, BLK), 0)
    total = 0
    for j in range(x_ref.shape[0]):
        start = start_ref[j, e]
        end = end_ref[j, e]
        total = total + (end - start)
        base = pl.multiple_of(jnp.minimum(start // 16 * 16, rows - window), 16)
        part = x_ref[j, pl.ds(base, window), :]
        keep = (place >= start - base) & (place < end - base)
        picked[pl.ds(j * window, window), :] = jnp.where(keep, part, jnp.zeros_like(part))
    left = picked[:, :HALF]
    right = picked[:, HALF:]

    def product(a, b):
        return lax.dot_general(a, b, (((0,), (0,)), ((), ())), preferred_element_type=jnp.float32)

    quarters = {(0, 0): product(left, left), (0, 1): product(left, right), (1, 1): product(right, right)}
    for n, (i, j) in enumerate(TILES):
        block = quarters[(i // 2, j // 2)]
        r, c = i % 2 * TILE, j % 2 * TILE
        o_ref[0, pl.ds(n * TILE, TILE), :] = block[r : r + TILE, c : c + TILE]
    o_ref[0, pl.ds(PACKED, 8), :] = jnp.full((8, TILE), total >> 5, jnp.int32).astype(jnp.float32)
    o_ref[0, pl.ds(PACKED + 8, 8), :] = jnp.full((8, TILE), total & 31, jnp.int32).astype(jnp.float32)


def gram(x, start, end, rows, most):
    sources = x.shape[0]
    height = PACKED + NOTE
    window = most + 16
    return pl.pallas_call(
        lambda *refs: gram_kernel(rows, window, *refs),
        grid_spec=pltpu.PrefetchScalarGridSpec(
            num_scalar_prefetch=2,
            grid=(EXPERTS,),
            in_specs=[pl.BlockSpec(memory_space=pltpu.VMEM)],
            out_specs=pl.BlockSpec((1, height, TILE), lambda e, s, t: (e, 0, 0)),
            scratch_shapes=[pltpu.VMEM((sources * window, BLK), jnp.bfloat16)],
        ),
        out_shape=jax.ShapeDtypeStruct((EXPERTS, height, TILE), jnp.float32),
        compiler_params=params(),
        cost_estimate=BRIEF,
    )(start, end, x)


def newton_kernel(packed, *refs):
    grams, o_ref = refs[:-7], refs[-7]
    e_top, e_low, x_top, x_low, f_ref, g_ref = refs[-6:]

    def diagonal(width):
        shape = (HALF, width)
        return lax.broadcasted_iota(jnp.int32, shape, 0) == lax.broadcasted_iota(jnp.int32, shape, 1)

    wide, square = diagonal(BLK), diagonal(HALF)

    def total(row, height):
        value = grams[0][pl.ds(row, height), :].astype(jnp.float32)
        for more in grams[1:]:
            value = value + more[pl.ds(row, height), :].astype(jnp.float32)
        return value

    note = total(PACKED, NOTE)
    scale = 1.0 / (32.0 * note[0:1, :] + note[8:9, :])
    for n, (i, j) in enumerate(TILES):
        tile = total(n * TILE, TILE) * scale
        if i < 2:
            e_top[pl.ds(i * TILE, TILE), pl.ds(j * TILE, TILE)] = tile
        else:
            e_low[pl.ds((i - 2) * TILE, TILE), pl.ds((j - 2) * TILE, TILE)] = tile
        if (i, j) == (0, 1):
            e_top[pl.ds(TILE, TILE), pl.ds(0, TILE)] = tile.T
        if (i, j) == (2, 3):
            e_low[pl.ds(TILE, TILE), pl.ds(0, TILE)] = tile.T
    top = e_top[...] + jnp.where(wide, DAMPING, 0.0)
    low = e_low[...] + jnp.where(square, DAMPING, 0.0)

    def squares(x):
        return jnp.sum(x * x, keepdims=True)

    norm = jnp.sqrt(squares(top[:, :HALF]) + 2.0 * squares(top[:, HALF:]) + squares(low))
    top, low = top / norm, low / norm
    e_top[...], e_low[...] = top, low
    x_top[...] = (jnp.where(wide, 2.0, 0.0) - top) / norm
    x_low[...] = (jnp.where(square, 2.0, 0.0) - low) / norm

    def center(top_ref, low_ref, whole):
        top, low = top_ref[...], low_ref[...]
        trace = jnp.sum(jnp.where(square, top[:, :HALF], 0.0) + jnp.where(square, low, 0.0), keepdims=True)
        mean = trace * (1.0 / BLK)
        top = top - jnp.where(wide, mean, 0.0)
        low = low - jnp.where(square, mean, 0.0)
        rounded = top.astype(jnp.bfloat16)
        whole[:HALF, :] = rounded
        whole[HALF:, HALF:] = low.astype(jnp.bfloat16)
        whole[HALF:, :HALF] = rounded[:, HALF:].T
        return mean, top, low

    def product(whole):
        return (
            jnp.dot(whole[:HALF, :], f_ref[...], preferred_element_type=jnp.float32),
            jnp.dot(whole[HALF:, :], f_ref[:, HALF:], preferred_element_type=jnp.float32),
        )

    def next_e(s, top, low):
        product_top, product_low = product(f_ref)
        e_top[...] = jnp.where(wide, 2.0 * s - s * s, 0.0) + (2.0 - 2.0 * s) * top - product_top
        e_low[...] = jnp.where(square, 2.0 * s - s * s, 0.0) + (2.0 - 2.0 * s) * low - product_low

    def next_x(s, e_top, e_low, t, top, low):
        product_top, product_low = product(g_ref)
        x_top[...] = jnp.where(wide, 2.0 * t - t * s, 0.0) + (2.0 - s) * top - t * e_top - product_top
        x_low[...] = jnp.where(square, 2.0 * t - t * s, 0.0) + (2.0 - s) * low - t * e_low - product_low

    next_e(*center(e_top, e_low, f_ref))
    for step in range(1, NS_STEPS):
        e = center(e_top, e_low, f_ref)
        x = center(x_top, x_low, g_ref)
        next_x(*e, *x)
        if step < NS_STEPS - 1:
            next_e(*e)
    top = x_top[...].astype(jnp.bfloat16)
    low = x_low[...].astype(jnp.bfloat16)
    if packed:
        for n, (i, j) in enumerate(TILES):
            rows = top if i < 2 else low
            r, c = i % 2 * TILE, (j if i < 2 else j - 2) * TILE
            o_ref[pl.ds(n * TILE, TILE), :] = rows[r : r + TILE, c : c + TILE]
    else:
        o_ref[:HALF, :] = top
        o_ref[HALF:, HALF:] = low
        o_ref[HALF:, :HALF] = top[:, HALF:].T


def newton(packed, *grams):
    return pl.pallas_call(
        lambda *refs: newton_kernel(packed, *refs),
        in_specs=[pl.BlockSpec(memory_space=pltpu.VMEM)] * len(grams),
        out_specs=pl.BlockSpec(memory_space=pltpu.VMEM),
        out_shape=jax.ShapeDtypeStruct((PACKED, TILE) if packed else (BLK, BLK), jnp.bfloat16),
        scratch_shapes=[pltpu.VMEM((HALF, BLK), jnp.float32), pltpu.VMEM((HALF, HALF), jnp.float32)] * 2
        + [pltpu.VMEM((BLK, BLK), jnp.bfloat16)] * 2,
        compiler_params=params(),
        cost_estimate=BRIEF,
    )(*grams)


def left_kernel(index_ref, *refs):
    packed, w_ref, o_ref, block = refs[:-3], refs[-3], refs[-2], refs[-1]
    for k, inverse in enumerate(packed):

        @pl.when(pl.program_id(0) == k)
        def _(inverse=inverse):
            for n, (i, j) in enumerate(TILES):
                tile = inverse[pl.ds(n * TILE, TILE), :]
                block[pl.ds(i * TILE, TILE), pl.ds(j * TILE, TILE)] = tile
                if i != j:
                    block[pl.ds(j * TILE, TILE), pl.ds(i * TILE, TILE)] = tile.T

    o_ref[...] = jnp.dot(
        block[...], w_ref[...], preferred_element_type=jnp.float32
    ).astype(jnp.bfloat16)


def left_product(index, packed, grad):
    blocks = len(packed)
    return pl.pallas_call(
        left_kernel,
        grid_spec=pltpu.PrefetchScalarGridSpec(
            num_scalar_prefetch=1,
            grid=(blocks,),
            in_specs=[pl.BlockSpec((PACKED, TILE), lambda n, s: (0, 0))] * blocks
            + [pl.BlockSpec((BLK, BLK), lambda n, s: (s[n], 0))],
            out_specs=pl.BlockSpec((BLK, BLK), lambda n, s: (s[n], 0)),
            scratch_shapes=[pltpu.VMEM((BLK, BLK), jnp.bfloat16)],
        ),
        out_shape=jax.ShapeDtypeStruct((blocks * BLK, BLK), jnp.bfloat16),
        compiler_params=params(),
        cost_estimate=BRIEF,
    )(index, *packed, grad)


def right_kernel(a_ref, b_ref, o_ref):
    o_ref[...] = jnp.dot(
        a_ref[...], b_ref[...], preferred_element_type=jnp.float32
    ).astype(jnp.bfloat16)


def right_product(a, b):
    blocks = a.shape[0] // BLK
    return pl.pallas_call(
        right_kernel,
        grid=(blocks,),
        in_specs=[
            pl.BlockSpec((BLK, BLK), lambda n: (n, 0)),
            pl.BlockSpec((BLK, BLK), lambda n: (0, 0)),
        ],
        out_specs=pl.BlockSpec((BLK, BLK), lambda n: (n, 0)),
        out_shape=jax.ShapeDtypeStruct((blocks * BLK, BLK), jnp.bfloat16),
        compiler_params=params(),
        cost_estimate=BRIEF,
    )(a, b)


def send(x, axis, target):
    return lax.ppermute(x, axis, [(i, target(i)) for i in range(lax.axis_size(axis))])


def sum_over_group(grams):
    return lax.psum_scatter(grams, "expert", scatter_dimension=0, tiled=True)[0]


def per_device(slot_inputs, slot_grads, slot_expert, weight_grad):
    shard_pos = lax.axis_index("shard")
    odd = shard_pos & 1
    ids_row = slot_expert.reshape(1, SLOT_DEV)
    sent_act = route(slot_inputs, slot_expert, ids_row, True)
    sent_out = route(slot_grads, slot_expert, ids_row, False)

    got_act = lax.all_to_all(sent_act, "shard", 0, 0, tiled=True)
    sent_out, got_act = lax.optimization_barrier((sent_out, got_act))
    got_out = lax.all_to_all(sent_out, "shard", 0, 0, tiled=True)

    counts = got_act[:, SLOT_DEV // 2, :EXPERTS].astype(jnp.int32)
    label = jnp.arange(EXPERTS, dtype=jnp.int32)
    before = (label[:, None] < label[None, :]).astype(jnp.int32)
    start = jnp.sum(counts[:, :, None] * before[None], axis=1)
    end = start + counts

    act = gram(got_act, (start + 1 - odd) >> 1, (end + 1 - odd) >> 1, SLOT_DEV // 2, CAP // 2)
    act = sum_over_group(act)
    out = sum_over_group(gram(got_out, start, end, SLOT_DEV, CAP))
    other = send(act.astype(jnp.bfloat16), "shard", lambda i: i ^ 1)
    act_inverse = newton(True, act, other)
    out_inverse = newton(False, out)

    def up(i):
        return (i + 4) % 16

    def down(i):
        return (i - 4) % 16

    across = send(act_inverse, "shard", lambda i: i // 4 * 4 + 3 - i % 4)
    own_below = send(act_inverse, "shard", up)
    own_above = send(act_inverse, "shard", down)
    across_below = send(across, "shard", up)
    across_above = send(across, "shard", down)
    own_far = send(own_below, "shard", up)
    across_far = send(across_above, "shard", down)
    z, side = shard_pos >> 2, shard_pos >> 1 & 1
    inverses = [act_inverse, across, own_below, across_below, own_above, across_above, own_far, across_far]
    index = []
    for step in (0, -1, 1, 2):
        index += [2 * ((z + step) & 3) + side, 2 * ((z + step) & 3) + 1 - side]
    left = left_product(jnp.stack(index).astype(jnp.int32), inverses, weight_grad[0])
    return right_product(left, out_inverse)[None]


def solution(mesh):
    in_specs = (
        P(("expert", "shard"), None),
        P(("expert", "shard"), None),
        P(("expert", "shard"), None),
        P("expert", None, "shard"),
    )
    out_specs = P("expert", None, "shard")
    return jax.shard_map(
        per_device, mesh=mesh, in_specs=in_specs, out_specs=out_specs, check_vma=False
    )
```

```python
import jax
import jax.numpy as jnp
from jax import lax
from jax.experimental import pallas as pl
from jax.experimental.pallas import tpu as pltpu
from jax.sharding import PartitionSpec as P

D = 4096
FF = 8192
BLK = 512
HALF = 256
TILE = 128
EXPERTS = 8
SLOT_DEV = 256
NS_STEPS = 8
DAMPING = 0.1
MIB = 1024 * 1024

TILES = [(i, j) for i in range(4) for j in range(i, 4)]
PACKED = len(TILES) * TILE
NOTE = 16
OUT_ROWS = SLOT_DEV // 2 + NOTE
CAP = 64

BRIEF = pl.CostEstimate(flops=1 << 20, bytes_accessed=1 << 12, transcendentals=0)


def params(mib):
    return pltpu.CompilerParams(vmem_limit_bytes=mib * MIB)


def route_kernel(col_ref, row_ref, inputs_ref, grads_ref, o_ref, halves, sorts):
    n = SLOT_DEV

    @pl.when(pl.program_id(0) == 0)
    def _():
        sub = lax.broadcasted_iota(jnp.int32, (n, n), 0)
        lane = lax.broadcasted_iota(jnp.int32, (n, n), 1)
        earlier = col_ref[...] * n + sub < row_ref[...] * n + lane
        place = jnp.sum(earlier.astype(jnp.float32), axis=0, keepdims=True)
        place = place.astype(jnp.int32)
        sorts[...] = (sub == place).astype(jnp.float32).astype(jnp.bfloat16)
        place = (place >> 1) + (place & 1) * (n // 2)
        halves[...] = (sub == place).astype(jnp.float32).astype(jnp.bfloat16)

    def moved(order, x):
        return jnp.dot(order[...], x, preferred_element_type=jnp.float32).astype(jnp.bfloat16)

    lane = lax.broadcasted_iota(jnp.int32, (n, BLK), 1)
    counts = jnp.sum((col_ref[...] == lane).astype(jnp.float32), axis=0, keepdims=True)
    counts = jnp.broadcast_to(counts, (NOTE, BLK)).astype(jnp.bfloat16)
    rows = moved(halves, inputs_ref[...])
    for half in range(2):
        o_ref[half, : n // 2, :] = rows[half * (n // 2) : (half + 1) * (n // 2)]
        o_ref[half, n // 2 : OUT_ROWS, :] = counts
        o_ref[half, OUT_ROWS:, :] = moved(sorts, grads_ref[:, half * BLK : (half + 1) * BLK])


def route(inputs, grads, ids_col, ids_row):
    pairs = inputs.shape[1] // BLK
    rows = OUT_ROWS + SLOT_DEV
    return pl.pallas_call(
        route_kernel,
        grid=(pairs,),
        in_specs=[
            pl.BlockSpec((SLOT_DEV, 1), lambda b: (0, 0)),
            pl.BlockSpec((1, SLOT_DEV), lambda b: (0, 0)),
            pl.BlockSpec((SLOT_DEV, BLK), lambda b: (0, b)),
            pl.BlockSpec((SLOT_DEV, 2 * BLK), lambda b: (0, b)),
        ],
        out_specs=pl.BlockSpec((2, rows, BLK), lambda b: (b, 0, 0)),
        out_shape=jax.ShapeDtypeStruct((2 * pairs, rows, BLK), jnp.bfloat16),
        scratch_shapes=[pltpu.VMEM((SLOT_DEV, SLOT_DEV), jnp.bfloat16)] * 2,
        compiler_params=params(20),
        cost_estimate=BRIEF,
    )(ids_col, ids_row, inputs, grads)


def gram_kernel(first, offset, rows, window, start_ref, end_ref, x_ref, o_ref, picked):
    e = pl.program_id(0) + first
    place = lax.broadcasted_iota(jnp.int32, (window, BLK), 0)
    total = 0
    for j in range(x_ref.shape[0]):
        start = start_ref[j, e]
        end = end_ref[j, e]
        total = total + (end - start)
        base = pl.multiple_of(jnp.minimum(start // 16 * 16, rows - window), 16)
        part = x_ref[j, pl.ds(offset + base, window), :]
        keep = (place >= start - base) & (place < end - base)
        picked[pl.ds(j * window, window), :] = jnp.where(keep, part, jnp.zeros_like(part))
    left = picked[:, :HALF]
    right = picked[:, HALF:]

    def product(a, b):
        return lax.dot_general(a, b, (((0,), (0,)), ((), ())), preferred_element_type=jnp.float32)

    quarters = {(0, 0): product(left, left), (0, 1): product(left, right), (1, 1): product(right, right)}
    for n, (i, j) in enumerate(TILES):
        block = quarters[(i // 2, j // 2)]
        r, c = i % 2 * TILE, j % 2 * TILE
        o_ref[0, pl.ds(n * TILE, TILE), :] = block[r : r + TILE, c : c + TILE]
    o_ref[0, pl.ds(PACKED, 8), :] = jnp.full((8, TILE), total >> 5, jnp.int32).astype(jnp.float32)
    o_ref[0, pl.ds(PACKED + 8, 8), :] = jnp.full((8, TILE), total & 31, jnp.int32).astype(jnp.float32)


def gram(x, start, end, first, offset, rows, most):
    sources = x.shape[0]
    height = PACKED + NOTE
    window = most + 16
    return pl.pallas_call(
        lambda *refs: gram_kernel(first, offset, rows, window, *refs),
        grid_spec=pltpu.PrefetchScalarGridSpec(
            num_scalar_prefetch=2,
            grid=(4,),
            in_specs=[pl.BlockSpec(memory_space=pltpu.VMEM)],
            out_specs=pl.BlockSpec((1, height, TILE), lambda e, s, t: (e, 0, 0)),
            scratch_shapes=[pltpu.VMEM((sources * window, BLK), jnp.bfloat16)],
        ),
        out_shape=jax.ShapeDtypeStruct((4, height, TILE), jnp.float32),
        compiler_params=params(20),
        cost_estimate=BRIEF,
    )(start, end, x)


def newton_kernel(packed, *refs):
    grams, o_ref = refs[:-7], refs[-7]
    e_top, e_low, x_top, x_low, f_ref, g_ref = refs[-6:]

    def diagonal(width):
        shape = (HALF, width)
        return lax.broadcasted_iota(jnp.int32, shape, 0) == lax.broadcasted_iota(jnp.int32, shape, 1)

    wide, square = diagonal(BLK), diagonal(HALF)

    def total(row, height):
        value = grams[0][pl.ds(row, height), :].astype(jnp.float32)
        for more in grams[1:]:
            value = value + more[pl.ds(row, height), :].astype(jnp.float32)
        return value

    note = total(PACKED, NOTE)
    scale = 1.0 / (32.0 * note[0:1, :] + note[8:9, :])
    for n, (i, j) in enumerate(TILES):
        tile = total(n * TILE, TILE) * scale
        if i < 2:
            e_top[pl.ds(i * TILE, TILE), pl.ds(j * TILE, TILE)] = tile
        else:
            e_low[pl.ds((i - 2) * TILE, TILE), pl.ds((j - 2) * TILE, TILE)] = tile
        if (i, j) == (0, 1):
            e_top[pl.ds(TILE, TILE), pl.ds(0, TILE)] = tile.T
        if (i, j) == (2, 3):
            e_low[pl.ds(TILE, TILE), pl.ds(0, TILE)] = tile.T
    top = e_top[...] + jnp.where(wide, DAMPING, 0.0)
    low = e_low[...] + jnp.where(square, DAMPING, 0.0)

    def squares(x):
        return jnp.sum(x * x, keepdims=True)

    norm = jnp.sqrt(squares(top[:, :HALF]) + 2.0 * squares(top[:, HALF:]) + squares(low))
    top, low = top / norm, low / norm
    e_top[...], e_low[...] = top, low
    x_top[...] = (jnp.where(wide, 2.0, 0.0) - top) / norm
    x_low[...] = (jnp.where(square, 2.0, 0.0) - low) / norm

    def center(top_ref, low_ref, whole):
        top, low = top_ref[...], low_ref[...]
        trace = jnp.sum(jnp.where(square, top[:, :HALF], 0.0) + jnp.where(square, low, 0.0), keepdims=True)
        mean = trace * (1.0 / BLK)
        top = top - jnp.where(wide, mean, 0.0)
        low = low - jnp.where(square, mean, 0.0)
        rounded = top.astype(jnp.bfloat16)
        whole[:HALF, :] = rounded
        whole[HALF:, HALF:] = low.astype(jnp.bfloat16)
        whole[HALF:, :HALF] = rounded[:, HALF:].T
        return mean, top, low

    def product(whole):
        return (
            jnp.dot(whole[:HALF, :], f_ref[...], preferred_element_type=jnp.float32),
            jnp.dot(whole[HALF:, :], f_ref[:, HALF:], preferred_element_type=jnp.float32),
        )

    def next_e(s, top, low):
        product_top, product_low = product(f_ref)
        e_top[...] = jnp.where(wide, 2.0 * s - s * s, 0.0) + (2.0 - 2.0 * s) * top - product_top
        e_low[...] = jnp.where(square, 2.0 * s - s * s, 0.0) + (2.0 - 2.0 * s) * low - product_low

    def next_x(s, e_top, e_low, t, top, low):
        product_top, product_low = product(g_ref)
        x_top[...] = jnp.where(wide, 2.0 * t - t * s, 0.0) + (2.0 - s) * top - t * e_top - product_top
        x_low[...] = jnp.where(square, 2.0 * t - t * s, 0.0) + (2.0 - s) * low - t * e_low - product_low

    next_e(*center(e_top, e_low, f_ref))
    for step in range(1, NS_STEPS):
        e = center(e_top, e_low, f_ref)
        x = center(x_top, x_low, g_ref)
        next_x(*e, *x)
        if step < NS_STEPS - 1:
            next_e(*e)
    top = x_top[...].astype(jnp.bfloat16)
    low = x_low[...].astype(jnp.bfloat16)
    if packed:
        for n, (i, j) in enumerate(TILES):
            rows = top if i < 2 else low
            r, c = i % 2 * TILE, (j if i < 2 else j - 2) * TILE
            o_ref[pl.ds(n * TILE, TILE), :] = rows[r : r + TILE, c : c + TILE]
    else:
        o_ref[:HALF, :] = top
        o_ref[HALF:, HALF:] = low
        o_ref[HALF:, :HALF] = top[:, HALF:].T


def newton(packed, *grams):
    return pl.pallas_call(
        lambda *refs: newton_kernel(packed, *refs),
        in_specs=[pl.BlockSpec(memory_space=pltpu.VMEM)] * len(grams),
        out_specs=pl.BlockSpec(memory_space=pltpu.VMEM),
        out_shape=jax.ShapeDtypeStruct((PACKED, TILE) if packed else (BLK, BLK), jnp.bfloat16),
        scratch_shapes=[pltpu.VMEM((HALF, BLK), jnp.float32), pltpu.VMEM((HALF, HALF), jnp.float32)] * 2
        + [pltpu.VMEM((BLK, BLK), jnp.bfloat16)] * 2,
        compiler_params=params(20),
        cost_estimate=BRIEF,
    )(*grams)


def unpack(packed, block):
    for n, (i, j) in enumerate(TILES):
        tile = packed[pl.ds(n * TILE, TILE), :]
        block[pl.ds(i * TILE, TILE), pl.ds(j * TILE, TILE)] = tile
        if i != j:
            block[pl.ds(j * TILE, TILE), pl.ds(i * TILE, TILE)] = tile.T


def left_kernel(count, index_ref, *refs):
    packed, w_hbm, o_ref, w_ref, block, w_sem = refs[:count], *refs[count:]

    def fetch(k):
        rows = pl.ds(pl.multiple_of(index_ref[k] * BLK, BLK), BLK)
        return pltpu.make_async_copy(w_hbm.at[rows], w_ref.at[k], w_sem.at[k])

    for k in range(count):
        fetch(k).start()
    for k in range(count):
        unpack(packed[k], block.at[k])
    for k in range(count):
        fetch(k).wait()
        left = jnp.dot(block[k], w_ref[k], preferred_element_type=jnp.float32)
        o_ref[k] = left.astype(jnp.bfloat16)


def left_product(index, packed, grad):
    count = len(packed)
    vmem = pl.BlockSpec(memory_space=pltpu.VMEM)
    return pl.pallas_call(
        lambda *refs: left_kernel(count, *refs),
        in_specs=[pl.BlockSpec(memory_space=pltpu.SMEM)]
        + [vmem] * count
        + [pl.BlockSpec(memory_space=pltpu.HBM)],
        out_specs=vmem,
        out_shape=jax.ShapeDtypeStruct((count, BLK, BLK), jnp.bfloat16),
        scratch_shapes=[pltpu.VMEM((count, BLK, BLK), jnp.bfloat16)] * 2
        + [pltpu.SemaphoreType.DMA((count,))],
        compiler_params=params(20),
        cost_estimate=BRIEF,
    )(index, *packed, grad)


def apply_kernel(count, index_ref, *refs):
    packed, (done_ref, w_hbm, right_ref, o_hbm) = refs[:count], refs[count : count + 4]
    w_ref, o_ref, block, w_sem, o_sem = refs[count + 4 :]
    first = done_ref.shape[0]

    def rows(k):
        return pl.ds(pl.multiple_of(index_ref[k] * BLK, BLK), BLK)

    def fetch(k):
        return pltpu.make_async_copy(w_hbm.at[rows(first + k)], w_ref.at[k], w_sem.at[k])

    def store(k):
        return pltpu.make_async_copy(o_ref.at[k], o_hbm.at[rows(k)], o_sem.at[k])

    def finish(k, left):
        o_ref[k] = jnp.dot(left, right_ref[...], preferred_element_type=jnp.float32).astype(jnp.bfloat16)
        store(k).start()

    for k in range(count):
        fetch(k).start()
    for k in range(first):
        finish(k, done_ref[k])
    for k in range(count):
        unpack(packed[k], block.at[k])
    for k in range(count):
        fetch(k).wait()
        left = jnp.dot(block[k], w_ref[k], preferred_element_type=jnp.float32)
        finish(first + k, left.astype(jnp.bfloat16))
    for k in range(first + count):
        store(k).wait()


def apply(index, done, packed, grad, right):
    count = len(packed)
    blocks = done.shape[0] + count
    vmem, hbm = pl.BlockSpec(memory_space=pltpu.VMEM), pl.BlockSpec(memory_space=pltpu.HBM)
    return pl.pallas_call(
        lambda *refs: apply_kernel(count, *refs),
        in_specs=[pl.BlockSpec(memory_space=pltpu.SMEM)] + [vmem] * count + [vmem, hbm, vmem],
        out_specs=hbm,
        out_shape=jax.ShapeDtypeStruct((blocks * BLK, BLK), jnp.bfloat16),
        scratch_shapes=[
            pltpu.VMEM((count, BLK, BLK), jnp.bfloat16),
            pltpu.VMEM((blocks, BLK, BLK), jnp.bfloat16),
            pltpu.VMEM((count, BLK, BLK), jnp.bfloat16),
            pltpu.SemaphoreType.DMA((count,)),
            pltpu.SemaphoreType.DMA((blocks,)),
        ],
        compiler_params=params(50),
        cost_estimate=BRIEF,
    )(index, *packed, done, grad, right)


def send(x, axis, target):
    return lax.ppermute(x, axis, [(i, target(i)) for i in range(lax.axis_size(axis))])


def sum_over_group(grams_of):
    got = send(grams_of(0), "expert", lambda i: i ^ 1)
    mine = grams_of(4)
    parts = [mine[0] + got[0]]
    for k in range(1, 4):
        part = (mine[k] + got[k]).astype(jnp.bfloat16)
        parts.append(send(part, "expert", lambda i: (i + 2 * k) % EXPERTS))
    return parts


def per_device(slot_inputs, slot_grads, slot_expert, weight_grad):
    shard_pos = lax.axis_index("shard")
    group_pos = lax.axis_index("expert")
    parity, group = group_pos & 1, group_pos >> 1
    odd = shard_pos & 1
    ids_row = slot_expert.reshape(1, SLOT_DEV)
    sent = route(slot_inputs, slot_grads, slot_expert, ids_row)
    sent, odd, parity, group, shard_pos = lax.optimization_barrier(
        (sent, odd, parity, group, shard_pos)
    )
    got = lax.all_to_all(sent, "shard", 0, 0, tiled=True)
    got, odd, parity, group, shard_pos, weight_grad = lax.optimization_barrier(
        (got, odd, parity, group, shard_pos, weight_grad)
    )

    counts = got[:, SLOT_DEV // 2, :EXPERTS].astype(jnp.int32)
    label = jnp.arange(EXPERTS, dtype=jnp.int32)
    order = 2 * ((group + label) & 3) + jnp.where(label < 4, 1 - parity, parity)
    before = (label[:, None] < order[None, :]).astype(jnp.int32)
    same = (label[:, None] == order[None, :]).astype(jnp.int32)
    start = jnp.sum(counts[:, :, None] * before[None], axis=1)
    end = start + jnp.sum(counts[:, :, None] * same[None], axis=1)

    own_start, own_end = (start + 1 - odd) >> 1, (end + 1 - odd) >> 1
    act_parts = sum_over_group(
        lambda first: gram(got, own_start, own_end, first, 0, SLOT_DEV // 2, CAP // 2)
    )
    act = act_parts[0]
    for part in act_parts[1:]:
        act = act + part.astype(jnp.float32)
    other = send(act.astype(jnp.bfloat16), "shard", lambda i: i ^ 1)
    act_inverse = newton(True, act, other)

    def up(i):
        return (i + 4) % 16

    def down(i):
        return (i - 4) % 16

    across = send(act_inverse, "shard", lambda i: i // 4 * 4 + 3 - i % 4)
    own_below = send(act_inverse, "shard", up)
    own_above = send(act_inverse, "shard", down)
    across_below = send(across, "shard", up)
    across_above = send(across, "shard", down)
    own_far = send(own_below, "shard", up)
    across_far = send(across_above, "shard", down)
    z, side = shard_pos >> 2, shard_pos >> 1 & 1
    early = [act_inverse, across, own_below, own_above]
    late = [across_below, across_above, own_far, across_far]
    places = [(0, 0), (0, 1), (-1, 0), (1, 0), (-1, 1), (1, 1), (2, 0), (2, 1)]
    index = [2 * ((z + step) & 3) + (side ^ other_side) for step, other_side in places]
    index = jnp.stack(index).astype(jnp.int32)

    out_parts = sum_over_group(lambda first: gram(got, start, end, first, OUT_ROWS, SLOT_DEV, CAP))
    done = left_product(index, early, weight_grad[0])
    out_inverse = newton(False, *out_parts)
    return apply(index, done, late, weight_grad[0], out_inverse)[None]


def solution(mesh):
    in_specs = (
        P(("expert", "shard"), None),
        P(("expert", "shard"), None),
        P(("expert", "shard"), None),
        P("expert", None, "shard"),
    )
    out_specs = P("expert", None, "shard")
    return jax.shard_map(
        per_device, mesh=mesh, in_specs=in_specs, out_specs=out_specs, check_vma=False
    )
```

```python
import jax
import jax.numpy as jnp
from jax import lax
from jax.experimental import pallas as pl
from jax.experimental.pallas import tpu as pltpu
from jax.sharding import PartitionSpec as P

D = 4096
FF = 8192
BLK = 512
HALF = 256
TILE = 128
EXPERTS = 8
SLOT_DEV = 256
NS_STEPS = 8
DAMPING = 0.1
MIB = 1024 * 1024

TILES = [(i, j) for i in range(4) for j in range(i, 4)]
PACKED = len(TILES) * TILE
NOTE = 16
OUT_ROWS = SLOT_DEV // 2 + NOTE
CAP = 64

BRIEF = pl.CostEstimate(flops=1 << 20, bytes_accessed=1 << 12, transcendentals=0)


def params(mib):
    return pltpu.CompilerParams(vmem_limit_bytes=mib * MIB)


def route_kernel(col_ref, row_ref, inputs_ref, grads_ref, o_ref, halves, sorts):
    n = SLOT_DEV

    @pl.when(pl.program_id(0) == 0)
    def _():
        sub = lax.broadcasted_iota(jnp.int32, (n, n), 0)
        lane = lax.broadcasted_iota(jnp.int32, (n, n), 1)
        earlier = col_ref[...] * n + sub < row_ref[...] * n + lane
        place = jnp.sum(earlier.astype(jnp.float32), axis=0, keepdims=True)
        place = place.astype(jnp.int32)
        sorts[...] = (sub == place).astype(jnp.float32).astype(jnp.bfloat16)
        place = (place >> 1) + (place & 1) * (n // 2)
        halves[...] = (sub == place).astype(jnp.float32).astype(jnp.bfloat16)

    def moved(order, x):
        return jnp.dot(order[...], x, preferred_element_type=jnp.float32).astype(jnp.bfloat16)

    lane = lax.broadcasted_iota(jnp.int32, (n, BLK), 1)
    counts = jnp.sum((col_ref[...] == lane).astype(jnp.float32), axis=0, keepdims=True)
    counts = jnp.broadcast_to(counts, (NOTE, BLK)).astype(jnp.bfloat16)
    rows = moved(halves, inputs_ref[...])
    for half in range(2):
        o_ref[half, : n // 2, :] = rows[half * (n // 2) : (half + 1) * (n // 2)]
        o_ref[half, n // 2 : OUT_ROWS, :] = counts
        o_ref[half, OUT_ROWS:, :] = moved(sorts, grads_ref[:, half * BLK : (half + 1) * BLK])


def route(inputs, grads, ids_col, ids_row):
    pairs = inputs.shape[1] // BLK
    rows = OUT_ROWS + SLOT_DEV
    return pl.pallas_call(
        route_kernel,
        grid=(pairs,),
        in_specs=[
            pl.BlockSpec((SLOT_DEV, 1), lambda b: (0, 0)),
            pl.BlockSpec((1, SLOT_DEV), lambda b: (0, 0)),
            pl.BlockSpec((SLOT_DEV, BLK), lambda b: (0, b)),
            pl.BlockSpec((SLOT_DEV, 2 * BLK), lambda b: (0, b)),
        ],
        out_specs=pl.BlockSpec((2, rows, BLK), lambda b: (b, 0, 0)),
        out_shape=jax.ShapeDtypeStruct((2 * pairs, rows, BLK), jnp.bfloat16),
        scratch_shapes=[pltpu.VMEM((SLOT_DEV, SLOT_DEV), jnp.bfloat16)] * 2,
        compiler_params=params(20),
        cost_estimate=BRIEF,
    )(ids_col, ids_row, inputs, grads)


def gram_kernel(first, offset, rows, window, start_ref, end_ref, x_ref, o_ref, picked):
    e = pl.program_id(0) + first
    place = lax.broadcasted_iota(jnp.int32, (window, BLK), 0)
    total = 0
    for j in range(x_ref.shape[0]):
        start = start_ref[j, e]
        end = end_ref[j, e]
        total = total + (end - start)
        base = pl.multiple_of(jnp.minimum(start // 16 * 16, rows - window), 16)
        part = x_ref[j, pl.ds(offset + base, window), :]
        keep = (place >= start - base) & (place < end - base)
        picked[pl.ds(j * window, window), :] = jnp.where(keep, part, jnp.zeros_like(part))
    left = picked[:, :HALF]
    right = picked[:, HALF:]

    def product(a, b):
        return lax.dot_general(a, b, (((0,), (0,)), ((), ())), preferred_element_type=jnp.float32)

    quarters = {(0, 0): product(left, left), (0, 1): product(left, right), (1, 1): product(right, right)}
    for n, (i, j) in enumerate(TILES):
        block = quarters[(i // 2, j // 2)]
        r, c = i % 2 * TILE, j % 2 * TILE
        o_ref[0, pl.ds(n * TILE, TILE), :] = block[r : r + TILE, c : c + TILE]
    o_ref[0, pl.ds(PACKED, 8), :] = jnp.full((8, TILE), total >> 5, jnp.int32).astype(jnp.float32)
    o_ref[0, pl.ds(PACKED + 8, 8), :] = jnp.full((8, TILE), total & 31, jnp.int32).astype(jnp.float32)


def gram(x, start, end, first, offset, rows, most):
    sources = x.shape[0]
    height = PACKED + NOTE
    window = most + 16
    return pl.pallas_call(
        lambda *refs: gram_kernel(first, offset, rows, window, *refs),
        grid_spec=pltpu.PrefetchScalarGridSpec(
            num_scalar_prefetch=2,
            grid=(4,),
            in_specs=[pl.BlockSpec(memory_space=pltpu.VMEM)],
            out_specs=pl.BlockSpec((1, height, TILE), lambda e, s, t: (e, 0, 0)),
            scratch_shapes=[pltpu.VMEM((sources * window, BLK), jnp.bfloat16)],
        ),
        out_shape=jax.ShapeDtypeStruct((4, height, TILE), jnp.float32),
        compiler_params=params(20),
        cost_estimate=BRIEF,
    )(start, end, x)


def newton_kernel(packed, *refs):
    grams, o_ref = refs[:-7], refs[-7]
    e_top, e_low, x_top, x_low, f_ref, g_ref = refs[-6:]

    def diagonal(width):
        shape = (HALF, width)
        return lax.broadcasted_iota(jnp.int32, shape, 0) == lax.broadcasted_iota(jnp.int32, shape, 1)

    wide, square = diagonal(BLK), diagonal(HALF)

    def total(row, height):
        value = grams[0][pl.ds(row, height), :].astype(jnp.float32)
        for more in grams[1:]:
            value = value + more[pl.ds(row, height), :].astype(jnp.float32)
        return value

    note = total(PACKED, NOTE)
    scale = 1.0 / (32.0 * note[0:1, :] + note[8:9, :])
    for n, (i, j) in enumerate(TILES):
        tile = total(n * TILE, TILE) * scale
        if i < 2:
            e_top[pl.ds(i * TILE, TILE), pl.ds(j * TILE, TILE)] = tile
        else:
            e_low[pl.ds((i - 2) * TILE, TILE), pl.ds((j - 2) * TILE, TILE)] = tile
        if (i, j) == (0, 1):
            e_top[pl.ds(TILE, TILE), pl.ds(0, TILE)] = tile.T
        if (i, j) == (2, 3):
            e_low[pl.ds(TILE, TILE), pl.ds(0, TILE)] = tile.T
    top = e_top[...] + jnp.where(wide, DAMPING, 0.0)
    low = e_low[...] + jnp.where(square, DAMPING, 0.0)

    def squares(x):
        return jnp.sum(x * x, keepdims=True)

    norm = jnp.sqrt(squares(top[:, :HALF]) + 2.0 * squares(top[:, HALF:]) + squares(low))
    top, low = top / norm, low / norm
    e_top[...], e_low[...] = top, low
    x_top[...] = (jnp.where(wide, 2.0, 0.0) - top) / norm
    x_low[...] = (jnp.where(square, 2.0, 0.0) - low) / norm

    def center(top_ref, low_ref, whole):
        top, low = top_ref[...], low_ref[...]
        trace = jnp.sum(jnp.where(square, top[:, :HALF], 0.0) + jnp.where(square, low, 0.0), keepdims=True)
        mean = trace * (1.0 / BLK)
        top = top - jnp.where(wide, mean, 0.0)
        low = low - jnp.where(square, mean, 0.0)
        rounded = top.astype(jnp.bfloat16)
        whole[:HALF, :] = rounded
        whole[HALF:, HALF:] = low.astype(jnp.bfloat16)
        whole[HALF:, :HALF] = rounded[:, HALF:].T
        return mean, top, low

    def product(whole):
        return (
            jnp.dot(whole[:HALF, :], f_ref[...], preferred_element_type=jnp.float32),
            jnp.dot(whole[HALF:, :], f_ref[:, HALF:], preferred_element_type=jnp.float32),
        )

    def next_e(s, top, low):
        product_top, product_low = product(f_ref)
        e_top[...] = jnp.where(wide, 2.0 * s - s * s, 0.0) + (2.0 - 2.0 * s) * top - product_top
        e_low[...] = jnp.where(square, 2.0 * s - s * s, 0.0) + (2.0 - 2.0 * s) * low - product_low

    def next_x(s, e_top, e_low, t, top, low):
        product_top, product_low = product(g_ref)
        x_top[...] = jnp.where(wide, 2.0 * t - t * s, 0.0) + (2.0 - s) * top - t * e_top - product_top
        x_low[...] = jnp.where(square, 2.0 * t - t * s, 0.0) + (2.0 - s) * low - t * e_low - product_low

    next_e(*center(e_top, e_low, f_ref))
    for step in range(1, NS_STEPS):
        e = center(e_top, e_low, f_ref)
        x = center(x_top, x_low, g_ref)
        next_x(*e, *x)
        if step < NS_STEPS - 1:
            next_e(*e)
    top = x_top[...].astype(jnp.bfloat16)
    low = x_low[...].astype(jnp.bfloat16)
    if packed:
        for n, (i, j) in enumerate(TILES):
            rows = top if i < 2 else low
            r, c = i % 2 * TILE, (j if i < 2 else j - 2) * TILE
            o_ref[pl.ds(n * TILE, TILE), :] = rows[r : r + TILE, c : c + TILE]
    else:
        o_ref[:HALF, :] = top
        o_ref[HALF:, HALF:] = low
        o_ref[HALF:, :HALF] = top[:, HALF:].T


def newton(packed, *grams):
    return pl.pallas_call(
        lambda *refs: newton_kernel(packed, *refs),
        in_specs=[pl.BlockSpec(memory_space=pltpu.VMEM)] * len(grams),
        out_specs=pl.BlockSpec(memory_space=pltpu.VMEM),
        out_shape=jax.ShapeDtypeStruct((PACKED, TILE) if packed else (BLK, BLK), jnp.bfloat16),
        scratch_shapes=[pltpu.VMEM((HALF, BLK), jnp.float32), pltpu.VMEM((HALF, HALF), jnp.float32)] * 2
        + [pltpu.VMEM((BLK, BLK), jnp.bfloat16)] * 2,
        compiler_params=params(20),
        cost_estimate=BRIEF,
    )(*grams)


def unpack(packed, block):
    for n, (i, j) in enumerate(TILES):
        tile = packed[pl.ds(n * TILE, TILE), :]
        block[pl.ds(i * TILE, TILE), pl.ds(j * TILE, TILE)] = tile
        if i != j:
            block[pl.ds(j * TILE, TILE), pl.ds(i * TILE, TILE)] = tile.T


def left_kernel(count, index_ref, *refs):
    packed, w_hbm, o_ref, w_ref, block, w_sem = refs[:count], *refs[count:]

    def fetch(k):
        rows = pl.ds(pl.multiple_of(index_ref[k] * BLK, BLK), BLK)
        return pltpu.make_async_copy(w_hbm.at[rows], w_ref.at[k], w_sem.at[k])

    for k in range(count):
        fetch(k).start()
    for k in range(count):
        unpack(packed[k], block.at[k])
    for k in range(count):
        fetch(k).wait()
        left = jnp.dot(block[k], w_ref[k], preferred_element_type=jnp.float32)
        o_ref[k] = left.astype(jnp.bfloat16)


def left_product(index, packed, grad):
    count = len(packed)
    vmem = pl.BlockSpec(memory_space=pltpu.VMEM)
    return pl.pallas_call(
        lambda *refs: left_kernel(count, *refs),
        in_specs=[pl.BlockSpec(memory_space=pltpu.SMEM)]
        + [vmem] * count
        + [pl.BlockSpec(memory_space=pltpu.HBM)],
        out_specs=vmem,
        out_shape=jax.ShapeDtypeStruct((count, BLK, BLK), jnp.bfloat16),
        scratch_shapes=[pltpu.VMEM((count, BLK, BLK), jnp.bfloat16)] * 2
        + [pltpu.SemaphoreType.DMA((count,))],
        compiler_params=params(20),
        cost_estimate=BRIEF,
    )(index, *packed, grad)


def apply_kernel(count, index_ref, *refs):
    packed, (done_ref, w_hbm, right_ref, o_hbm) = refs[:count], refs[count : count + 4]
    w_ref, o_ref, block, w_sem, o_sem = refs[count + 4 :]
    first = done_ref.shape[0]

    def rows(k):
        return pl.ds(pl.multiple_of(index_ref[k] * BLK, BLK), BLK)

    def fetch(k):
        return pltpu.make_async_copy(w_hbm.at[rows(first + k)], w_ref.at[k], w_sem.at[k])

    def store(k):
        return pltpu.make_async_copy(o_ref.at[k], o_hbm.at[rows(k)], o_sem.at[k])

    def finish(k, left):
        o_ref[k] = jnp.dot(left, right_ref[...], preferred_element_type=jnp.float32).astype(jnp.bfloat16)
        store(k).start()

    for k in range(count):
        fetch(k).start()
    for k in range(first):
        finish(k, done_ref[k])
    for k in range(count):
        unpack(packed[k], block.at[k])
    for k in range(count):
        fetch(k).wait()
        left = jnp.dot(block[k], w_ref[k], preferred_element_type=jnp.float32)
        finish(first + k, left.astype(jnp.bfloat16))
    for k in range(first + count):
        store(k).wait()


def apply(index, done, packed, grad, right):
    count = len(packed)
    blocks = done.shape[0] + count
    vmem, hbm = pl.BlockSpec(memory_space=pltpu.VMEM), pl.BlockSpec(memory_space=pltpu.HBM)
    return pl.pallas_call(
        lambda *refs: apply_kernel(count, *refs),
        in_specs=[pl.BlockSpec(memory_space=pltpu.SMEM)] + [vmem] * count + [vmem, hbm, vmem],
        out_specs=hbm,
        out_shape=jax.ShapeDtypeStruct((blocks * BLK, BLK), jnp.bfloat16),
        scratch_shapes=[
            pltpu.VMEM((count, BLK, BLK), jnp.bfloat16),
            pltpu.VMEM((blocks, BLK, BLK), jnp.bfloat16),
            pltpu.VMEM((count, BLK, BLK), jnp.bfloat16),
            pltpu.SemaphoreType.DMA((count,)),
            pltpu.SemaphoreType.DMA((blocks,)),
        ],
        compiler_params=params(50),
        cost_estimate=BRIEF,
    )(index, *packed, done, grad, right)


def send(x, axis, target):
    return lax.ppermute(x, axis, [(i, target(i)) for i in range(lax.axis_size(axis))])


def sum_over_chip(grams_of):
    got = send(grams_of(0), "expert", lambda i: i ^ 1)
    mine = grams_of(4)
    return [mine[0] + got[0]] + [(mine[k] + got[k]).astype(jnp.bfloat16) for k in range(1, 4)]


def exchange_along_y(parts):
    return parts[:1] + [
        send(part, "expert", lambda i, k=k: (i + 2 * k) % EXPERTS)
        for k, part in enumerate(parts[1:], 1)
    ]


def per_device(slot_inputs, slot_grads, slot_expert, weight_grad):
    shard_pos = lax.axis_index("shard")
    group_pos = lax.axis_index("expert")
    parity, group = group_pos & 1, group_pos >> 1
    odd = shard_pos & 1
    ids_row = slot_expert.reshape(1, SLOT_DEV)
    sent = route(slot_inputs, slot_grads, slot_expert, ids_row)
    sent, odd, parity, group, shard_pos = lax.optimization_barrier(
        (sent, odd, parity, group, shard_pos)
    )
    got = lax.all_to_all(sent, "shard", 0, 0, tiled=True)
    got, odd, parity, group, shard_pos, weight_grad = lax.optimization_barrier(
        (got, odd, parity, group, shard_pos, weight_grad)
    )

    counts = got[:, SLOT_DEV // 2, :EXPERTS].astype(jnp.int32)
    label = jnp.arange(EXPERTS, dtype=jnp.int32)
    order = 2 * ((group + label) & 3) + jnp.where(label < 4, 1 - parity, parity)
    before = (label[:, None] < order[None, :]).astype(jnp.int32)
    same = (label[:, None] == order[None, :]).astype(jnp.int32)
    start = jnp.sum(counts[:, :, None] * before[None], axis=1)
    end = start + jnp.sum(counts[:, :, None] * same[None], axis=1)

    own_start, own_end = (start + 1 - odd) >> 1, (end + 1 - odd) >> 1
    act_parts = sum_over_chip(
        lambda first: gram(got, own_start, own_end, first, 0, SLOT_DEV // 2, CAP // 2)
    )
    act_parts = exchange_along_y(act_parts)
    out_parts = sum_over_chip(lambda first: gram(got, start, end, first, OUT_ROWS, SLOT_DEV, CAP))
    act = act_parts[0]
    for part in act_parts[1:]:
        act = act + part.astype(jnp.float32)
    other = send(act.astype(jnp.bfloat16), "shard", lambda i: i ^ 1)
    other, _ = lax.optimization_barrier((other, out_parts))
    act_inverse = newton(True, act, other)
    out_parts = exchange_along_y(out_parts)

    def up(i):
        return (i + 4) % 16

    def down(i):
        return (i - 4) % 16

    across = send(act_inverse, "shard", lambda i: i // 4 * 4 + 3 - i % 4)
    across, out_parts = lax.optimization_barrier((across, out_parts))
    own_below = send(act_inverse, "shard", up)
    own_above = send(act_inverse, "shard", down)
    across_below = send(across, "shard", up)
    across_above = send(across, "shard", down)
    own_far = send(own_below, "shard", up)
    out_inverse = newton(False, *out_parts)
    across_above, out_inverse = lax.optimization_barrier((across_above, out_inverse))
    across_far = send(across_above, "shard", down)
    z, side = shard_pos >> 2, shard_pos >> 1 & 1
    places = [(0, 0), (0, 1), (1, 1), (-1, 0), (1, 0), (-1, 1), (2, 0), (2, 1)]
    index = [2 * ((z + step) & 3) + (side ^ other_side) for step, other_side in places]
    index = jnp.stack(index).astype(jnp.int32)

    early = [act_inverse, across, across_above]
    done = left_product(index, early, weight_grad[0])
    late = [own_below, own_above, across_below, own_far, across_far]
    return apply(index, done, late, weight_grad[0], out_inverse)[None]


def solution(mesh):
    in_specs = (
        P(("expert", "shard"), None),
        P(("expert", "shard"), None),
        P(("expert", "shard"), None),
        P("expert", None, "shard"),
    )
    out_specs = P("expert", None, "shard")
    return jax.shard_map(
        per_device, mesh=mesh, in_specs=in_specs, out_specs=out_specs, check_vma=False
    )
```

```python
import jax
import jax.numpy as jnp
from jax import lax
from jax.experimental import pallas as pl
from jax.experimental.pallas import tpu as pltpu
from jax.sharding import PartitionSpec as P

D = 4096
FF = 8192
BLK = 512
HALF = 256
TILE = 128
EXPERTS = 8
SLOT_DEV = 256
NS_STEPS = 8
DAMPING = 0.1
MIB = 1024 * 1024

TILES = [(i, j) for i in range(4) for j in range(i, 4)]
PACKED = len(TILES) * TILE
NOTE = 16
OUT_ROWS = SLOT_DEV // 2 + NOTE
CAP = 64

BRIEF = pl.CostEstimate(flops=1 << 20, bytes_accessed=1 << 12, transcendentals=0)


def params(mib):
    return pltpu.CompilerParams(vmem_limit_bytes=mib * MIB)


def route_kernel(row_ref, inputs_ref, grads_ref, o_ref, halves, sorts, counts):
    n = SLOT_DEV

    @pl.when(pl.program_id(0) == 0)
    def _():
        sub = lax.broadcasted_iota(jnp.int32, (n, n), 0)
        lane = lax.broadcasted_iota(jnp.int32, (n, n), 1)
        ids = jnp.broadcast_to(row_ref[...].astype(jnp.float32), (n, n))
        column = ids.T
        earlier = (column < ids) | ((column == ids) & (sub < lane))
        place = jnp.sum(earlier.astype(jnp.float32), axis=0, keepdims=True)
        place = place.astype(jnp.int32)
        sorts[...] = (sub == place).astype(jnp.float32).astype(jnp.bfloat16)
        place = (place >> 1) + (place & 1) * (n // 2)
        halves[...] = (sub == place).astype(jnp.float32).astype(jnp.bfloat16)
        named = (column == lane.astype(jnp.float32)).astype(jnp.float32)
        totals = jnp.broadcast_to(jnp.sum(named, axis=0, keepdims=True), (NOTE, n))
        counts[...] = jnp.concatenate([totals, totals], axis=1).astype(jnp.bfloat16)

    def moved(order, x):
        return jnp.dot(order[...], x, preferred_element_type=jnp.float32).astype(jnp.bfloat16)

    rows = moved(halves, inputs_ref[...])
    for half in range(2):
        o_ref[half, : n // 2, :] = rows[half * (n // 2) : (half + 1) * (n // 2)]
        o_ref[half, n // 2 : OUT_ROWS, :] = counts[...]
        o_ref[half, OUT_ROWS:, :] = moved(sorts, grads_ref[:, half * BLK : (half + 1) * BLK])


def route(inputs, grads, ids_row):
    pairs = inputs.shape[1] // BLK
    rows = OUT_ROWS + SLOT_DEV
    return pl.pallas_call(
        route_kernel,
        grid=(pairs,),
        in_specs=[
            pl.BlockSpec((1, SLOT_DEV), lambda b: (0, 0)),
            pl.BlockSpec((SLOT_DEV, BLK), lambda b: (0, b)),
            pl.BlockSpec((SLOT_DEV, 2 * BLK), lambda b: (0, b)),
        ],
        out_specs=pl.BlockSpec((2, rows, BLK), lambda b: (b, 0, 0)),
        out_shape=jax.ShapeDtypeStruct((2 * pairs, rows, BLK), jnp.bfloat16),
        scratch_shapes=[pltpu.VMEM((SLOT_DEV, SLOT_DEV), jnp.bfloat16)] * 2
        + [pltpu.VMEM((NOTE, BLK), jnp.bfloat16)],
        compiler_params=params(20),
        cost_estimate=BRIEF,
    )(ids_row, inputs, grads)


def gram_kernel(first, offset, rows, window, start_ref, end_ref, x_ref, o_ref, picked):
    e = pl.program_id(0) + first
    place = lax.broadcasted_iota(jnp.int32, (window, BLK), 0)
    total = 0
    for j in range(x_ref.shape[0]):
        start = start_ref[j, e]
        end = end_ref[j, e]
        total = total + (end - start)
        base = pl.multiple_of(jnp.minimum(start // 16 * 16, rows - window), 16)
        part = x_ref[j, pl.ds(offset + base, window), :]
        keep = (place >= start - base) & (place < end - base)
        picked[pl.ds(j * window, window), :] = jnp.where(keep, part, jnp.zeros_like(part))
    left = picked[:, :HALF]
    right = picked[:, HALF:]

    def product(a, b):
        return lax.dot_general(a, b, (((0,), (0,)), ((), ())), preferred_element_type=jnp.float32)

    quarters = {(0, 0): product(left, left), (0, 1): product(left, right), (1, 1): product(right, right)}
    for n, (i, j) in enumerate(TILES):
        block = quarters[(i // 2, j // 2)]
        r, c = i % 2 * TILE, j % 2 * TILE
        o_ref[0, pl.ds(n * TILE, TILE), :] = block[r : r + TILE, c : c + TILE]
    o_ref[0, pl.ds(PACKED, 8), :] = jnp.full((8, TILE), total >> 5, jnp.int32).astype(jnp.float32)
    o_ref[0, pl.ds(PACKED + 8, 8), :] = jnp.full((8, TILE), total & 31, jnp.int32).astype(jnp.float32)


def gram(x, start, end, first, offset, rows, most):
    sources = x.shape[0]
    height = PACKED + NOTE
    window = most + 16
    return pl.pallas_call(
        lambda *refs: gram_kernel(first, offset, rows, window, *refs),
        grid_spec=pltpu.PrefetchScalarGridSpec(
            num_scalar_prefetch=2,
            grid=(4,),
            in_specs=[pl.BlockSpec(memory_space=pltpu.VMEM)],
            out_specs=pl.BlockSpec((1, height, TILE), lambda e, s, t: (e, 0, 0)),
            scratch_shapes=[pltpu.VMEM((sources * window, BLK), jnp.bfloat16)],
        ),
        out_shape=jax.ShapeDtypeStruct((4, height, TILE), jnp.float32),
        compiler_params=params(20),
        cost_estimate=BRIEF,
    )(start, end, x)


def newton_kernel(packed, *refs):
    grams, o_ref = refs[:-7], refs[-7]
    e_top, e_low, x_top, x_low, f_ref, g_ref = refs[-6:]

    def diagonal(width):
        shape = (HALF, width)
        return lax.broadcasted_iota(jnp.int32, shape, 0) == lax.broadcasted_iota(jnp.int32, shape, 1)

    wide, square = diagonal(BLK), diagonal(HALF)

    def total(row, height):
        value = grams[0][pl.ds(row, height), :].astype(jnp.float32)
        for more in grams[1:]:
            value = value + more[pl.ds(row, height), :].astype(jnp.float32)
        return value

    note = total(PACKED, NOTE)
    scale = 1.0 / (32.0 * note[0:1, :] + note[8:9, :])
    for n, (i, j) in enumerate(TILES):
        tile = total(n * TILE, TILE) * scale
        if i < 2:
            e_top[pl.ds(i * TILE, TILE), pl.ds(j * TILE, TILE)] = tile
        else:
            e_low[pl.ds((i - 2) * TILE, TILE), pl.ds((j - 2) * TILE, TILE)] = tile
        if (i, j) == (0, 1):
            e_top[pl.ds(TILE, TILE), pl.ds(0, TILE)] = tile.T
        if (i, j) == (2, 3):
            e_low[pl.ds(TILE, TILE), pl.ds(0, TILE)] = tile.T
    top = e_top[...] + jnp.where(wide, DAMPING, 0.0)
    low = e_low[...] + jnp.where(square, DAMPING, 0.0)

    def squares(x):
        return jnp.sum(x * x, keepdims=True)

    norm = jnp.sqrt(squares(top[:, :HALF]) + 2.0 * squares(top[:, HALF:]) + squares(low))
    top, low = top / norm, low / norm
    e_top[...], e_low[...] = top, low
    x_top[...] = (jnp.where(wide, 2.0, 0.0) - top) / norm
    x_low[...] = (jnp.where(square, 2.0, 0.0) - low) / norm

    def center(top_ref, low_ref, whole):
        top, low = top_ref[...], low_ref[...]
        trace = jnp.sum(jnp.where(square, top[:, :HALF], 0.0) + jnp.where(square, low, 0.0), keepdims=True)
        mean = trace * (1.0 / BLK)
        top = top - jnp.where(wide, mean, 0.0)
        low = low - jnp.where(square, mean, 0.0)
        rounded = top.astype(jnp.bfloat16)
        whole[:HALF, :] = rounded
        whole[HALF:, HALF:] = low.astype(jnp.bfloat16)
        whole[HALF:, :HALF] = rounded[:, HALF:].T
        return mean, top, low

    def product(whole):
        return (
            jnp.dot(whole[:HALF, :], f_ref[...], preferred_element_type=jnp.float32),
            jnp.dot(whole[HALF:, :], f_ref[:, HALF:], preferred_element_type=jnp.float32),
        )

    def next_e(s, top, low):
        product_top, product_low = product(f_ref)
        e_top[...] = jnp.where(wide, 2.0 * s - s * s, 0.0) + (2.0 - 2.0 * s) * top - product_top
        e_low[...] = jnp.where(square, 2.0 * s - s * s, 0.0) + (2.0 - 2.0 * s) * low - product_low

    def next_x(s, e_top, e_low, t, top, low):
        product_top, product_low = product(g_ref)
        x_top[...] = jnp.where(wide, 2.0 * t - t * s, 0.0) + (2.0 - s) * top - t * e_top - product_top
        x_low[...] = jnp.where(square, 2.0 * t - t * s, 0.0) + (2.0 - s) * low - t * e_low - product_low

    next_e(*center(e_top, e_low, f_ref))
    for step in range(1, NS_STEPS):
        e = center(e_top, e_low, f_ref)
        x = center(x_top, x_low, g_ref)
        next_x(*e, *x)
        if step < NS_STEPS - 1:
            next_e(*e)
    top = x_top[...].astype(jnp.bfloat16)
    low = x_low[...].astype(jnp.bfloat16)
    if packed:
        for n, (i, j) in enumerate(TILES):
            rows = top if i < 2 else low
            r, c = i % 2 * TILE, (j if i < 2 else j - 2) * TILE
            o_ref[pl.ds(n * TILE, TILE), :] = rows[r : r + TILE, c : c + TILE]
    else:
        o_ref[:HALF, :] = top
        o_ref[HALF:, HALF:] = low
        o_ref[HALF:, :HALF] = top[:, HALF:].T


def newton(packed, *grams):
    return pl.pallas_call(
        lambda *refs: newton_kernel(packed, *refs),
        in_specs=[pl.BlockSpec(memory_space=pltpu.VMEM)] * len(grams),
        out_specs=pl.BlockSpec(memory_space=pltpu.VMEM),
        out_shape=jax.ShapeDtypeStruct((PACKED, TILE) if packed else (BLK, BLK), jnp.bfloat16),
        scratch_shapes=[pltpu.VMEM((HALF, BLK), jnp.float32), pltpu.VMEM((HALF, HALF), jnp.float32)] * 2
        + [pltpu.VMEM((BLK, BLK), jnp.bfloat16)] * 2,
        compiler_params=params(20),
        cost_estimate=BRIEF,
    )(*grams)


def unpack(packed, block):
    for n, (i, j) in enumerate(TILES):
        tile = packed[pl.ds(n * TILE, TILE), :]
        block[pl.ds(i * TILE, TILE), pl.ds(j * TILE, TILE)] = tile
        if i != j:
            block[pl.ds(j * TILE, TILE), pl.ds(i * TILE, TILE)] = tile.T


def left_kernel(count, index_ref, *refs):
    packed, w_hbm, o_ref, w_ref, block, w_sem = refs[:count], *refs[count:]

    def fetch(k):
        rows = pl.ds(pl.multiple_of(index_ref[k] * BLK, BLK), BLK)
        return pltpu.make_async_copy(w_hbm.at[rows], w_ref.at[k], w_sem.at[k])

    for k in range(count):
        fetch(k).start()
    for k in range(count):
        unpack(packed[k], block.at[k])
    for k in range(count):
        fetch(k).wait()
        left = jnp.dot(block[k], w_ref[k], preferred_element_type=jnp.float32)
        o_ref[k] = left.astype(jnp.bfloat16)


def left_product(index, packed, grad):
    count = len(packed)
    vmem = pl.BlockSpec(memory_space=pltpu.VMEM)
    return pl.pallas_call(
        lambda *refs: left_kernel(count, *refs),
        in_specs=[pl.BlockSpec(memory_space=pltpu.SMEM)]
        + [vmem] * count
        + [pl.BlockSpec(memory_space=pltpu.HBM)],
        out_specs=vmem,
        out_shape=jax.ShapeDtypeStruct((count, BLK, BLK), jnp.bfloat16),
        scratch_shapes=[pltpu.VMEM((count, BLK, BLK), jnp.bfloat16)] * 2
        + [pltpu.SemaphoreType.DMA((count,))],
        compiler_params=params(20),
        cost_estimate=BRIEF,
    )(index, *packed, grad)


def apply_kernel(count, index_ref, *refs):
    packed, (done_ref, w_hbm, right_ref, o_hbm) = refs[:count], refs[count : count + 4]
    w_ref, o_ref, block, w_sem, o_sem = refs[count + 4 :]
    first = done_ref.shape[0]

    def rows(k):
        return pl.ds(pl.multiple_of(index_ref[k] * BLK, BLK), BLK)

    def fetch(k):
        return pltpu.make_async_copy(w_hbm.at[rows(first + k)], w_ref.at[k], w_sem.at[k])

    def store(k):
        return pltpu.make_async_copy(o_ref.at[k], o_hbm.at[rows(k)], o_sem.at[k])

    def finish(k, left):
        o_ref[k] = jnp.dot(left, right_ref[...], preferred_element_type=jnp.float32).astype(jnp.bfloat16)
        store(k).start()

    for k in range(count):
        fetch(k).start()
    for k in range(first):
        finish(k, done_ref[k])
    for k in range(count):
        unpack(packed[k], block.at[k])
    for k in range(count):
        fetch(k).wait()
        left = jnp.dot(block[k], w_ref[k], preferred_element_type=jnp.float32)
        finish(first + k, left.astype(jnp.bfloat16))
    for k in range(first + count):
        store(k).wait()


def apply(index, done, packed, grad, right):
    count = len(packed)
    blocks = done.shape[0] + count
    vmem, hbm = pl.BlockSpec(memory_space=pltpu.VMEM), pl.BlockSpec(memory_space=pltpu.HBM)
    return pl.pallas_call(
        lambda *refs: apply_kernel(count, *refs),
        in_specs=[pl.BlockSpec(memory_space=pltpu.SMEM)] + [vmem] * count + [vmem, hbm, vmem],
        out_specs=hbm,
        out_shape=jax.ShapeDtypeStruct((blocks * BLK, BLK), jnp.bfloat16),
        scratch_shapes=[
            pltpu.VMEM((count, BLK, BLK), jnp.bfloat16),
            pltpu.VMEM((blocks, BLK, BLK), jnp.bfloat16),
            pltpu.VMEM((count, BLK, BLK), jnp.bfloat16),
            pltpu.SemaphoreType.DMA((count,)),
            pltpu.SemaphoreType.DMA((blocks,)),
        ],
        compiler_params=params(50),
        cost_estimate=BRIEF,
    )(index, *packed, done, grad, right)


def send(x, axis, target):
    return lax.ppermute(x, axis, [(i, target(i)) for i in range(lax.axis_size(axis))])


def sum_over_chip(grams_of):
    got = send(grams_of(0), "expert", lambda i: i ^ 1)
    mine = grams_of(4)
    return [mine[0] + got[0]] + [(mine[k] + got[k]).astype(jnp.bfloat16) for k in range(1, 4)]


def exchange_along_y(parts):
    return parts[:1] + [
        send(part, "expert", lambda i, k=k: (i + 2 * k) % EXPERTS)
        for k, part in enumerate(parts[1:], 1)
    ]


def per_device(slot_inputs, slot_grads, slot_expert, weight_grad):
    shard_pos = lax.axis_index("shard")
    group_pos = lax.axis_index("expert")
    parity, group = group_pos & 1, group_pos >> 1
    odd = shard_pos & 1
    ids_row = slot_expert.reshape(1, SLOT_DEV)
    sent = route(slot_inputs, slot_grads, ids_row)
    sent, odd, parity, group, shard_pos = lax.optimization_barrier(
        (sent, odd, parity, group, shard_pos)
    )
    got = lax.all_to_all(sent, "shard", 0, 0, tiled=True)
    got, odd, parity, group, shard_pos, weight_grad = lax.optimization_barrier(
        (got, odd, parity, group, shard_pos, weight_grad)
    )

    counts = got[:, SLOT_DEV // 2, :EXPERTS].astype(jnp.int32)
    label = jnp.arange(EXPERTS, dtype=jnp.int32)
    order = 2 * ((group + label) & 3) + jnp.where(label < 4, 1 - parity, parity)
    before = (label[:, None] < order[None, :]).astype(jnp.int32)
    same = (label[:, None] == order[None, :]).astype(jnp.int32)
    start = jnp.sum(counts[:, :, None] * before[None], axis=1)
    end = start + jnp.sum(counts[:, :, None] * same[None], axis=1)

    own_start, own_end = (start + 1 - odd) >> 1, (end + 1 - odd) >> 1
    act_parts = sum_over_chip(
        lambda first: gram(got, own_start, own_end, first, 0, SLOT_DEV // 2, CAP // 2)
    )
    act_parts = exchange_along_y(act_parts)
    out_parts = sum_over_chip(lambda first: gram(got, start, end, first, OUT_ROWS, SLOT_DEV, CAP))
    act = act_parts[0]
    for part in act_parts[1:]:
        act = act + part.astype(jnp.float32)
    other = send(act.astype(jnp.bfloat16), "shard", lambda i: i ^ 1)
    other, _ = lax.optimization_barrier((other, out_parts))
    act_inverse = newton(True, act, other)
    out_parts = exchange_along_y(out_parts)

    def up(i):
        return (i + 4) % 16

    def down(i):
        return (i - 4) % 16

    across = send(act_inverse, "shard", lambda i: i // 4 * 4 + 3 - i % 4)
    across, out_parts = lax.optimization_barrier((across, out_parts))
    own_below = send(act_inverse, "shard", up)
    own_above = send(act_inverse, "shard", down)
    across_below = send(across, "shard", up)
    across_above = send(across, "shard", down)
    own_far = send(own_below, "shard", up)
    out_inverse = newton(False, *out_parts)
    across_above, out_inverse = lax.optimization_barrier((across_above, out_inverse))
    across_far = send(across_above, "shard", down)
    z, side = shard_pos >> 2, shard_pos >> 1 & 1
    places = [(0, 0), (0, 1), (1, 1), (-1, 0), (1, 0), (-1, 1), (2, 0), (2, 1)]
    index = [2 * ((z + step) & 3) + (side ^ other_side) for step, other_side in places]
    index = jnp.stack(index).astype(jnp.int32)

    early = [act_inverse, across, across_above]
    done = left_product(index, early, weight_grad[0])
    late = [own_below, own_above, across_below, own_far, across_far]
    return apply(index, done, late, weight_grad[0], out_inverse)[None]


def solution(mesh):
    in_specs = (
        P(("expert", "shard"), None),
        P(("expert", "shard"), None),
        P(("expert", "shard"), None),
        P("expert", None, "shard"),
    )
    out_specs = P("expert", None, "shard")
    return jax.shard_map(
        per_device, mesh=mesh, in_specs=in_specs, out_specs=out_specs, check_vma=False
    )
```

```python
import jax
import jax.numpy as jnp
from jax import lax
from jax.experimental import pallas as pl
from jax.experimental.pallas import tpu as pltpu
from jax.sharding import PartitionSpec as P

D = 4096
FF = 8192
BLK = 512
HALF = 256
TILE = 128
EXPERTS = 8
SLOT_DEV = 256
NS_STEPS = 8
DAMPING = 0.1
MIB = 1024 * 1024

TILES = [(i, j) for i in range(4) for j in range(i, 4)]
PACKED = len(TILES) * TILE
NOTE = 16
OUT_ROWS = SLOT_DEV // 2 + NOTE
CAP = 64

BRIEF = pl.CostEstimate(flops=1 << 20, bytes_accessed=1 << 12, transcendentals=0)


def params(mib):
    return pltpu.CompilerParams(vmem_limit_bytes=mib * MIB)


def route_kernel(row_ref, inputs_ref, grads_ref, o_ref, halves, sorts, counts):
    n = SLOT_DEV

    @pl.when(pl.program_id(0) == 0)
    def _():
        sub = lax.broadcasted_iota(jnp.int32, (n, n), 0)
        lane = lax.broadcasted_iota(jnp.int32, (n, n), 1)
        ids = jnp.broadcast_to(row_ref[...].astype(jnp.float32), (n, n))
        column = ids.T
        earlier = (column < ids) | ((column == ids) & (sub < lane))
        place = jnp.sum(earlier.astype(jnp.float32), axis=0, keepdims=True)
        place = place.astype(jnp.int32)
        sorts[...] = (sub == place).astype(jnp.float32).astype(jnp.bfloat16)
        place = (place >> 1) + (place & 1) * (n // 2)
        halves[...] = (sub == place).astype(jnp.float32).astype(jnp.bfloat16)
        named = (column == lane.astype(jnp.float32)).astype(jnp.float32)
        totals = jnp.broadcast_to(jnp.sum(named, axis=0, keepdims=True), (NOTE, n))
        counts[...] = jnp.concatenate([totals, totals], axis=1).astype(jnp.bfloat16)

    def moved(order, x):
        return jnp.dot(order[...], x, preferred_element_type=jnp.float32).astype(jnp.bfloat16)

    rows = moved(halves, inputs_ref[...])
    for half in range(2):
        o_ref[half, : n // 2, :] = rows[half * (n // 2) : (half + 1) * (n // 2)]
        o_ref[half, n // 2 : OUT_ROWS, :] = counts[...]
        o_ref[half, OUT_ROWS:, :] = moved(sorts, grads_ref[:, half * BLK : (half + 1) * BLK])


def route(inputs, grads, ids_row):
    pairs = inputs.shape[1] // BLK
    rows = OUT_ROWS + SLOT_DEV
    return pl.pallas_call(
        route_kernel,
        grid=(pairs,),
        in_specs=[
            pl.BlockSpec((1, SLOT_DEV), lambda b: (0, 0)),
            pl.BlockSpec((SLOT_DEV, BLK), lambda b: (0, b)),
            pl.BlockSpec((SLOT_DEV, 2 * BLK), lambda b: (0, b)),
        ],
        out_specs=pl.BlockSpec((2, rows, BLK), lambda b: (b, 0, 0)),
        out_shape=jax.ShapeDtypeStruct((2 * pairs, rows, BLK), jnp.bfloat16),
        scratch_shapes=[pltpu.VMEM((SLOT_DEV, SLOT_DEV), jnp.bfloat16)] * 2
        + [pltpu.VMEM((NOTE, BLK), jnp.bfloat16)],
        compiler_params=params(20),
        cost_estimate=BRIEF,
    )(ids_row, inputs, grads)


def gram_kernel(first, offset, rows, window, start_ref, end_ref, x_ref, o_ref, picked):
    e = pl.program_id(0) + first
    place = lax.broadcasted_iota(jnp.int32, (window, BLK), 0)
    total = 0
    for j in range(x_ref.shape[0]):
        start = start_ref[j, e]
        end = end_ref[j, e]
        total = total + (end - start)
        base = pl.multiple_of(jnp.minimum(start // 16 * 16, rows - window), 16)
        part = x_ref[j, pl.ds(offset + base, window), :]
        keep = (place >= start - base) & (place < end - base)
        picked[pl.ds(j * window, window), :] = jnp.where(keep, part, jnp.zeros_like(part))
    left = picked[:, :HALF]
    right = picked[:, HALF:]

    def product(a, b):
        return lax.dot_general(a, b, (((0,), (0,)), ((), ())), preferred_element_type=jnp.float32)

    upper = product(left, picked[...])
    quarters = {(0, 0): upper[:, :HALF], (0, 1): upper[:, HALF:], (1, 1): product(right, right)}
    for n, (i, j) in enumerate(TILES):
        block = quarters[(i // 2, j // 2)]
        r, c = i % 2 * TILE, j % 2 * TILE
        o_ref[0, pl.ds(n * TILE, TILE), :] = block[r : r + TILE, c : c + TILE]
    o_ref[0, pl.ds(PACKED, 8), :] = jnp.full((8, TILE), total >> 5, jnp.int32).astype(jnp.float32)
    o_ref[0, pl.ds(PACKED + 8, 8), :] = jnp.full((8, TILE), total & 31, jnp.int32).astype(jnp.float32)


def gram(x, start, end, first, offset, rows, most):
    sources = x.shape[0]
    height = PACKED + NOTE
    window = most + 16
    return pl.pallas_call(
        lambda *refs: gram_kernel(first, offset, rows, window, *refs),
        grid_spec=pltpu.PrefetchScalarGridSpec(
            num_scalar_prefetch=2,
            grid=(4,),
            in_specs=[pl.BlockSpec(memory_space=pltpu.VMEM)],
            out_specs=pl.BlockSpec((1, height, TILE), lambda e, s, t: (e, 0, 0)),
            scratch_shapes=[pltpu.VMEM((sources * window, BLK), jnp.bfloat16)],
        ),
        out_shape=jax.ShapeDtypeStruct((4, height, TILE), jnp.float32),
        compiler_params=params(20),
        cost_estimate=BRIEF,
    )(start, end, x)


def newton_kernel(packed, *refs):
    grams, o_ref = refs[:-7], refs[-7]
    e_top, e_low, x_top, x_low, f_ref, g_ref = refs[-6:]

    def diagonal(width):
        shape = (HALF, width)
        return lax.broadcasted_iota(jnp.int32, shape, 0) == lax.broadcasted_iota(jnp.int32, shape, 1)

    wide, square = diagonal(BLK), diagonal(HALF)

    def total(row, height):
        value = grams[0][pl.ds(row, height), :].astype(jnp.float32)
        for more in grams[1:]:
            value = value + more[pl.ds(row, height), :].astype(jnp.float32)
        return value

    note = total(PACKED, NOTE)
    scale = 1.0 / (32.0 * note[0:1, :] + note[8:9, :])
    for n, (i, j) in enumerate(TILES):
        tile = total(n * TILE, TILE) * scale
        if i < 2:
            e_top[pl.ds(i * TILE, TILE), pl.ds(j * TILE, TILE)] = tile
        else:
            e_low[pl.ds((i - 2) * TILE, TILE), pl.ds((j - 2) * TILE, TILE)] = tile
        if (i, j) == (0, 1):
            e_top[pl.ds(TILE, TILE), pl.ds(0, TILE)] = tile.T
        if (i, j) == (2, 3):
            e_low[pl.ds(TILE, TILE), pl.ds(0, TILE)] = tile.T
    top = e_top[...] + jnp.where(wide, DAMPING, 0.0)
    low = e_low[...] + jnp.where(square, DAMPING, 0.0)

    def squares(x):
        return jnp.sum(x * x, keepdims=True)

    norm = jnp.sqrt(squares(top[:, :HALF]) + 2.0 * squares(top[:, HALF:]) + squares(low))
    top, low = top / norm, low / norm
    e_top[...], e_low[...] = top, low
    x_top[...] = (jnp.where(wide, 2.0, 0.0) - top) / norm
    x_low[...] = (jnp.where(square, 2.0, 0.0) - low) / norm

    def center(top_ref, low_ref, whole):
        top, low = top_ref[...], low_ref[...]
        trace = jnp.sum(jnp.where(square, top[:, :HALF], 0.0) + jnp.where(square, low, 0.0), keepdims=True)
        mean = trace * (1.0 / BLK)
        top = top - jnp.where(wide, mean, 0.0)
        low = low - jnp.where(square, mean, 0.0)
        rounded = top.astype(jnp.bfloat16)
        whole[:HALF, :] = rounded
        whole[HALF:, HALF:] = low.astype(jnp.bfloat16)
        whole[HALF:, :HALF] = rounded[:, HALF:].T
        return mean, top, low

    def product(whole):
        return (
            jnp.dot(whole[:HALF, :], f_ref[...], preferred_element_type=jnp.float32),
            jnp.dot(whole[HALF:, :], f_ref[:, HALF:], preferred_element_type=jnp.float32),
        )

    def next_e(s, top, low):
        product_top, product_low = product(f_ref)
        e_top[...] = jnp.where(wide, 2.0 * s - s * s, 0.0) + (2.0 - 2.0 * s) * top - product_top
        e_low[...] = jnp.where(square, 2.0 * s - s * s, 0.0) + (2.0 - 2.0 * s) * low - product_low

    def next_x(s, e_top, e_low, t, top, low):
        product_top, product_low = product(g_ref)
        x_top[...] = jnp.where(wide, 2.0 * t - t * s, 0.0) + (2.0 - s) * top - t * e_top - product_top
        x_low[...] = jnp.where(square, 2.0 * t - t * s, 0.0) + (2.0 - s) * low - t * e_low - product_low

    next_e(*center(e_top, e_low, f_ref))
    for step in range(1, NS_STEPS):
        e = center(e_top, e_low, f_ref)
        x = center(x_top, x_low, g_ref)
        next_x(*e, *x)
        if step < NS_STEPS - 1:
            next_e(*e)
    top = x_top[...].astype(jnp.bfloat16)
    low = x_low[...].astype(jnp.bfloat16)
    if packed:
        for n, (i, j) in enumerate(TILES):
            rows = top if i < 2 else low
            r, c = i % 2 * TILE, (j if i < 2 else j - 2) * TILE
            o_ref[pl.ds(n * TILE, TILE), :] = rows[r : r + TILE, c : c + TILE]
    else:
        o_ref[:HALF, :] = top
        o_ref[HALF:, HALF:] = low
        o_ref[HALF:, :HALF] = top[:, HALF:].T


def newton(packed, *grams):
    return pl.pallas_call(
        lambda *refs: newton_kernel(packed, *refs),
        in_specs=[pl.BlockSpec(memory_space=pltpu.VMEM)] * len(grams),
        out_specs=pl.BlockSpec(memory_space=pltpu.VMEM),
        out_shape=jax.ShapeDtypeStruct((PACKED, TILE) if packed else (BLK, BLK), jnp.bfloat16),
        scratch_shapes=[pltpu.VMEM((HALF, BLK), jnp.float32), pltpu.VMEM((HALF, HALF), jnp.float32)] * 2
        + [pltpu.VMEM((BLK, BLK), jnp.bfloat16)] * 2,
        compiler_params=params(20),
        cost_estimate=BRIEF,
    )(*grams)


def unpack(packed, block):
    for n, (i, j) in enumerate(TILES):
        tile = packed[pl.ds(n * TILE, TILE), :]
        block[pl.ds(i * TILE, TILE), pl.ds(j * TILE, TILE)] = tile
        if i != j:
            block[pl.ds(j * TILE, TILE), pl.ds(i * TILE, TILE)] = tile.T


def left_kernel(count, index_ref, *refs):
    packed, w_hbm, o_ref, w_ref, block, w_sem = refs[:count], *refs[count:]

    def fetch(k):
        rows = pl.ds(pl.multiple_of(index_ref[k] * BLK, BLK), BLK)
        return pltpu.make_async_copy(w_hbm.at[rows], w_ref.at[k], w_sem.at[k])

    for k in range(count):
        fetch(k).start()
    for k in range(count):
        unpack(packed[k], block.at[k])
    for k in range(count):
        fetch(k).wait()
        left = jnp.dot(block[k], w_ref[k], preferred_element_type=jnp.float32)
        o_ref[k] = left.astype(jnp.bfloat16)


def left_product(index, packed, grad):
    count = len(packed)
    vmem = pl.BlockSpec(memory_space=pltpu.VMEM)
    return pl.pallas_call(
        lambda *refs: left_kernel(count, *refs),
        in_specs=[pl.BlockSpec(memory_space=pltpu.SMEM)]
        + [vmem] * count
        + [pl.BlockSpec(memory_space=pltpu.HBM)],
        out_specs=vmem,
        out_shape=jax.ShapeDtypeStruct((count, BLK, BLK), jnp.bfloat16),
        scratch_shapes=[pltpu.VMEM((count, BLK, BLK), jnp.bfloat16)] * 2
        + [pltpu.SemaphoreType.DMA((count,))],
        compiler_params=params(20),
        cost_estimate=BRIEF,
    )(index, *packed, grad)


def apply_kernel(count, index_ref, *refs):
    packed, (done_ref, w_hbm, right_ref, o_hbm) = refs[:count], refs[count : count + 4]
    w_ref, o_ref, block, w_sem, o_sem = refs[count + 4 :]
    first = done_ref.shape[0]

    def rows(k):
        return pl.ds(pl.multiple_of(index_ref[k] * BLK, BLK), BLK)

    def fetch(k):
        return pltpu.make_async_copy(w_hbm.at[rows(first + k)], w_ref.at[k], w_sem.at[k])

    def store(k):
        return pltpu.make_async_copy(o_ref.at[k], o_hbm.at[rows(k)], o_sem.at[k])

    def finish(k, left):
        o_ref[k] = jnp.dot(left, right_ref[...], preferred_element_type=jnp.float32).astype(jnp.bfloat16)
        store(k).start()

    for k in range(count):
        fetch(k).start()
    for k in range(first):
        finish(k, done_ref[k])
    for k in range(count):
        unpack(packed[k], block.at[k])
    for k in range(count):
        fetch(k).wait()
        left = jnp.dot(block[k], w_ref[k], preferred_element_type=jnp.float32)
        finish(first + k, left.astype(jnp.bfloat16))
    for k in range(first + count):
        store(k).wait()


def apply(index, done, packed, grad, right):
    count = len(packed)
    blocks = done.shape[0] + count
    vmem, hbm = pl.BlockSpec(memory_space=pltpu.VMEM), pl.BlockSpec(memory_space=pltpu.HBM)
    return pl.pallas_call(
        lambda *refs: apply_kernel(count, *refs),
        in_specs=[pl.BlockSpec(memory_space=pltpu.SMEM)] + [vmem] * count + [vmem, hbm, vmem],
        out_specs=hbm,
        out_shape=jax.ShapeDtypeStruct((blocks * BLK, BLK), jnp.bfloat16),
        scratch_shapes=[
            pltpu.VMEM((count, BLK, BLK), jnp.bfloat16),
            pltpu.VMEM((blocks, BLK, BLK), jnp.bfloat16),
            pltpu.VMEM((count, BLK, BLK), jnp.bfloat16),
            pltpu.SemaphoreType.DMA((count,)),
            pltpu.SemaphoreType.DMA((blocks,)),
        ],
        compiler_params=params(50),
        cost_estimate=BRIEF,
    )(index, *packed, done, grad, right)


def send(x, axis, target):
    return lax.ppermute(x, axis, [(i, target(i)) for i in range(lax.axis_size(axis))])


def sum_over_chip(grams_of):
    got = send(grams_of(0), "expert", lambda i: i ^ 1)
    mine = grams_of(4)
    return [mine[0] + got[0]] + [(mine[k] + got[k]).astype(jnp.bfloat16) for k in range(1, 4)]


def exchange_along_y(parts):
    return parts[:1] + [
        send(part, "expert", lambda i, k=k: (i + 2 * k) % EXPERTS)
        for k, part in enumerate(parts[1:], 1)
    ]


def per_device(slot_inputs, slot_grads, slot_expert, weight_grad):
    shard_pos = lax.axis_index("shard")
    group_pos = lax.axis_index("expert")
    parity, group = group_pos & 1, group_pos >> 1
    odd = shard_pos & 1
    ids_row = slot_expert.reshape(1, SLOT_DEV)
    sent = route(slot_inputs, slot_grads, ids_row)
    sent, odd, parity, group, shard_pos = lax.optimization_barrier(
        (sent, odd, parity, group, shard_pos)
    )
    got = lax.all_to_all(sent, "shard", 0, 0, tiled=True)
    got, odd, parity, group, shard_pos, weight_grad = lax.optimization_barrier(
        (got, odd, parity, group, shard_pos, weight_grad)
    )

    counts = got[:, SLOT_DEV // 2, :EXPERTS].astype(jnp.int32)
    label = jnp.arange(EXPERTS, dtype=jnp.int32)
    order = 2 * ((group + label) & 3) + jnp.where(label < 4, 1 - parity, parity)
    before = (label[:, None] < order[None, :]).astype(jnp.int32)
    same = (label[:, None] == order[None, :]).astype(jnp.int32)
    start = jnp.sum(counts[:, :, None] * before[None], axis=1)
    end = start + jnp.sum(counts[:, :, None] * same[None], axis=1)

    own_start, own_end = (start + 1 - odd) >> 1, (end + 1 - odd) >> 1
    act_parts = sum_over_chip(
        lambda first: gram(got, own_start, own_end, first, 0, SLOT_DEV // 2, CAP // 2)
    )
    act_parts = exchange_along_y(act_parts)
    out_parts = sum_over_chip(lambda first: gram(got, start, end, first, OUT_ROWS, SLOT_DEV, CAP))
    act = act_parts[0]
    for part in act_parts[1:]:
        act = act + part.astype(jnp.float32)
    other = send(act.astype(jnp.bfloat16), "shard", lambda i: i ^ 1)
    other, _ = lax.optimization_barrier((other, out_parts))
    act_inverse = newton(True, act, other)
    out_parts = exchange_along_y(out_parts)

    def up(i):
        return (i + 4) % 16

    def down(i):
        return (i - 4) % 16

    across = send(act_inverse, "shard", lambda i: i // 4 * 4 + 3 - i % 4)
    across, out_parts = lax.optimization_barrier((across, out_parts))
    own_below = send(act_inverse, "shard", up)
    own_above = send(act_inverse, "shard", down)
    across_below = send(across, "shard", up)
    across_above = send(across, "shard", down)
    own_far = send(own_below, "shard", up)
    out_inverse = newton(False, *out_parts)
    across_above, out_inverse = lax.optimization_barrier((across_above, out_inverse))
    across_far = send(across_above, "shard", down)
    z, side = shard_pos >> 2, shard_pos >> 1 & 1
    places = [(0, 0), (0, 1), (1, 1), (-1, 0), (1, 0), (-1, 1), (2, 0), (2, 1)]
    index = [2 * ((z + step) & 3) + (side ^ other_side) for step, other_side in places]
    index = jnp.stack(index).astype(jnp.int32)

    early = [act_inverse, across, across_above]
    done = left_product(index, early, weight_grad[0])
    late = [own_below, own_above, across_below, own_far, across_far]
    return apply(index, done, late, weight_grad[0], out_inverse)[None]


def solution(mesh):
    in_specs = (
        P(("expert", "shard"), None),
        P(("expert", "shard"), None),
        P(("expert", "shard"), None),
        P("expert", None, "shard"),
    )
    out_specs = P("expert", None, "shard")
    return jax.shard_map(
        per_device, mesh=mesh, in_specs=in_specs, out_specs=out_specs, check_vma=False
    )
```
